32 devices in a mesh: exp: 8 (over z, y), ccd: 4 (over x, core).
Axes of the slice: x: 2, y: 2, z: 4, core: 2. Of those that a mesh axis runs over, the one named last changes fastest.
Arguments:
- science: float32 [8, 256, 128], P('exp', 'ccd'), may hold values from -6 to 6
- variance: float32 [8, 256, 128], P('exp', 'ccd'), may hold values from 0.25 to 4
- template: bfloat16 [8, 256, 128], P('exp', 'ccd'), may hold values from -6 to 6
- kernel_coeff: float32 [8, 4, 40], P('exp', 'ccd'), may hold values from -1.8 to 1.8
- template_shift: int32 [8, 4], P('exp', 'ccd'), may hold values from 10 to 118
- corner_rows: int32 [8, 4, 256], P('exp', 'ccd'), may hold values from 0 to 32
- corner_cols: int32 [8, 4, 256], P('exp', 'ccd'), may hold values from 0 to 96
- owner_device: int32 [8, 4, 256, 1], P('exp', 'ccd'), may hold values from 0 to 31; in each aligned block of 256 rows (0 to 255, 256 to 511, ..., all dimensions but the last counted through in order) at most 16 rows name the same one
- object_slot: int32 [8, 4, 256], P('exp', 'ccd'), may hold values from 0 to 127
Outputs:
- object_stamps: float32 [4096, 1024], P(('exp', 'ccd'))
The draws below stay inside these ranges and needn't reach their ends.
Inputs may be any that keep to these rules, and one draw needn't show every extreme that they name: `owner_device`: among the 256 sources of one tile, no owner is named more than 16 times; some owner is named exactly 16 times.
All inputs are finite; a program needn't handle non-finite values.
Results may differ from the reference program's by a relative error of at most 0.0052.
Values may be sent and summed in bfloat16 or wider, within the bound.
A program may use at most 64 MiB of HBM per device.

```python
import math
import jax
import jax.numpy as jnp
import numpy as np
from jax import lax

ROWS = 64
COLS = 128
NB = 40
KW = 21
CUT = 32
SRC = 256
OBJ_DEV = 128
NEXP = 8
NCCD = 4
DEVS = 32
CAP = 16
OBJECTS = 4096


def with_ends(entries, key, low, high):
    dims = entries.shape
    place = [jax.random.randint(jax.random.fold_in(key, axis), (), 0, dims[axis]) for axis in range(len(dims))]
    entries = entries.at[tuple(place)].set(low)
    longest = dims.index(max(dims))
    place[longest] = (place[longest] + 1) % dims[longest]
    return entries.at[tuple(place)].set(high)


def steps_of(rng, shape, shards, low, largest):
    factor_of, own = 1.0, jax.random.fold_in(rng, 6)
    for dim, blocks in shards:
        steps = jnp.exp(jax.random.uniform(jax.random.fold_in(own, dim), (blocks,), jnp.float32, low / len(shards), largest / len(shards)))
        factor_of = factor_of * jnp.repeat(steps, shape[dim] // blocks).reshape([-1 if axis == dim else 1 for axis in range(len(shape))])
    return factor_of


def routed_block(stream_key, own, number, rows, amount, top, reach, lean):
    ranking = jax.random.permutation(stream_key, amount)
    crowded, common = load_shares(amount, rows * top, reach, lean, True), load_shares(amount, rows * top, reach, lean, False)
    places = jnp.arange(amount)

    def named(tallies, offset_by):
        used = int((tallies > 0).sum())
        fixed = max(1, used // 4)
        passed = fixed + (places - fixed + offset_by * (used - fixed)) % max(1, amount - fixed)
        return jnp.zeros((amount,), jnp.int32).at[ranking[jnp.where(places < fixed, places, passed)]].set(jnp.asarray(tallies, jnp.int32))

    tallies = jnp.where(number % 4 == 0, named(crowded, number // 4), named(common, number - number // 4 - 1))
    mixed = jax.random.permutation(jax.random.fold_in(own, 3), amount)
    source_of, receiver = mixed[0:amount // 2 * 2:2], mixed[1:amount // 2 * 2:2]
    slack = jnp.minimum(tallies[source_of] - 1, reach - tallies[receiver]) // 2
    slack = jnp.where((source_of == ranking[0]) | (receiver == ranking[0]) | (tallies[receiver] == 0), 0, jnp.maximum(slack, 0))
    passed = jax.random.randint(jax.random.fold_in(own, 4), (amount // 2,), 0, 1 << 20) % (slack + 1)
    tallies = tallies.at[source_of].add(-passed).at[receiver].add(passed)
    members = jnp.searchsorted(jnp.cumsum(tallies), jnp.arange(rows * top), side="right").astype(jnp.int32)
    listing = members.reshape(top, rows).T
    listing = listing[jax.random.permutation(jax.random.fold_in(own, 1), rows)]
    offset_by = jax.random.randint(jax.random.fold_in(own, 2), (rows, 1), 0, top)
    return jnp.take_along_axis(listing, (jnp.arange(top)[None, :] + offset_by) % top, axis=1)


def load_shares(count, total, most, skew, full):
    portions = [(1 << 20) // math.isqrt(grade ** skew) + 1 for grade in range(1, count + 1)]
    largest = most if full else min(most, max(-(-total // count), total * portions[0] // sum(portions)))
    least = 1 if total - largest >= count - 1 else 0
    given, rest = [largest] + [least] * (count - 1), total - largest - least * (count - 1)
    while rest > 0:
        candidates = [i for i in range(1, count) if given[i] < largest] or [i for i in range(1, count) if given[i] < most]
        pool, budget = sum([portions[i] for i in candidates]), rest
        for i in candidates:
            addition = min(most - given[i], max(1, budget * portions[i] // pool), rest)
            given[i] = given[i] + addition
            rest = rest - addition
    return np.array(given)


def normal_values(key, extent, scale, reach, split=(), kind=jnp.bfloat16):
    gain = steps_of(key, extent, split, -0.22, 0.18) if split else 1.0
    array = jax.random.normal(key, extent, jnp.float32) * scale * gain
    return jnp.minimum(jnp.maximum(array, -reach), reach).astype(kind)


def setup_inputs(seed: int = 0) -> dict:
    seeds = jax.random.split(jax.random.key(seed), 10)
    science = normal_values(seeds[0], (NEXP, NCCD * ROWS, COLS), 1.0, 6.0, ((0, 8), (1, 4)), jnp.float32)
    variance = jnp.clip(jnp.exp(math.log(4.0) - 2.7725887 * jax.random.uniform(seeds[1], (NEXP, NCCD * ROWS, COLS), jnp.float32) ** steps_of(seeds[1], (NEXP, NCCD * ROWS, COLS), ((0, 8), (1, 4)), -0.2, 0.2)), 0.25, 4.0)
    template = normal_values(seeds[2], (NEXP, NCCD * ROWS, COLS), 1.0, 6.0, ((0, 8), (1, 4)))
    kernel_coeff = normal_values(seeds[3], (NEXP, NCCD, NB), 0.3, 1.8, ((0, 8), (1, 4)), jnp.float32)
    template_shift = with_ends(jax.random.randint(seeds[4], (NEXP, NCCD), KW // 2, COLS - KW // 2 + 1), jax.random.fold_in(seeds[4], 1), KW // 2, (COLS - KW // 2 + 1) - 1).astype(jnp.int32)
    corner_rows = with_ends(jax.random.randint(seeds[5], (NEXP, NCCD, SRC), 0, ROWS - CUT + 1), jax.random.fold_in(seeds[5], 1), 0, ROWS - CUT).astype(jnp.int32)
    corner_cols = with_ends(jax.random.randint(seeds[6], (NEXP, NCCD, SRC), 0, COLS - CUT + 1), jax.random.fold_in(seeds[6], 1), 0, COLS - CUT).astype(jnp.int32)
    owner_device_keys = jax.random.split(jax.random.fold_in(seeds[7], 1), NEXP * NCCD * SRC // SRC)
    owner_device_turns = jax.random.permutation(jax.random.fold_in(seeds[7], 3), NEXP * NCCD * SRC // SRC)
    owner_device = jax.vmap(lambda own, number: routed_block(jax.random.fold_in(seeds[7], 2), own, number, SRC, DEVS, 1, CAP, 2))(owner_device_keys, owner_device_turns).reshape((NEXP, NCCD, SRC, 1))
    object_slot = with_ends(jax.random.randint(seeds[8], (NEXP, NCCD, SRC), 0, OBJ_DEV), jax.random.fold_in(seeds[8], 1), 0, OBJ_DEV - 1).astype(jnp.int32)
    return {"science": science, "variance": variance, "template": template, "kernel_coeff": kernel_coeff, "template_shift": template_shift, "corner_rows": corner_rows, "corner_cols": corner_cols, "owner_device": owner_device, "object_slot": object_slot}


def basis_profiles(count, width):
    middle = width // 2
    offsets = np.arange(width) - middle
    sigmas = (1.0, 2.0, 3.5)
    across = np.zeros((count, width))
    down = np.zeros((count, width))
    for basis in range(count):
        sigma = sigmas[min(basis // 16, 2)]
        scaled = offsets / sigma
        envelope = np.exp(-0.5 * scaled * scaled)
        first = scaled ** (basis % 4) * envelope
        second = scaled ** (basis // 4 % 4) * envelope
        across[basis] = first / np.sqrt(np.sum(first * first))
        down[basis] = second / np.sqrt(np.sum(second * second))
    return (across, down)

def column_table(across, span):
    count, width = across.shape
    table = np.zeros((span + width - 1, count * span))
    for basis in range(count):
        for column in range(span):
            table[column:column + width, basis * span + column] = across[basis]
    return table

def row_table(down, span):
    count, width = down.shape
    table = np.zeros((span, count, span + width - 1))
    for row in range(span):
        table[row, :, row:row + width] = down
    return table

def convolve(window, coeff):
    count = coeff.shape[0]
    width = KW
    tile_rows = window.shape[0] - width + 1
    tile_cols = window.shape[1] - width + 1
    row_span = min(tile_rows, 128)
    col_span = 128
    across, down = basis_profiles(count, width)
    col_weights = jnp.asarray(column_table(across, col_span)).astype(jnp.float32).astype(jnp.bfloat16)
    row_weights = (jnp.asarray(row_table(down, row_span)).astype(jnp.float32) * coeff[None, :, None]).astype(jnp.bfloat16)
    pieces = []
    for column_start in range(0, tile_cols, col_span):
        strip = window[:, column_start:column_start + col_span + width - 1]
        smeared = jnp.dot(strip, col_weights, preferred_element_type=jnp.float32).astype(jnp.bfloat16)
        smeared = smeared.reshape(strip.shape[0], count, col_span)
        parts = []
        for row_start in range(0, tile_rows, row_span):
            band = smeared[row_start:row_start + row_span + width - 1]
            parts.append(jnp.einsum('ibk,kbj->ij', row_weights.astype(jnp.float32), band.astype(jnp.float32), precision=lax.Precision.HIGHEST))
        pieces.append(jnp.concatenate(parts, axis=0))
    return jnp.concatenate(pieces, axis=1)

def cut_stamps(snr, top_rows, left_cols):

    def single(top, left):
        return lax.dynamic_slice(snr, (top, left), (CUT, CUT)).reshape(CUT * CUT)
    return jax.vmap(single)(top_rows, left_cols).astype(jnp.bfloat16)

def reference(science, variance, template, kernel_coeff, template_shift, corner_rows, corner_cols, owner_device, object_slot):
    margin = KW // 2
    padded = jnp.pad(template, ((0, 0), (margin, margin), (0, 0)))
    stripe = jnp.concatenate([padded, jnp.roll(padded, -1, axis=0)], axis=2)

    def visit(carry, device):
        sums, counts = carry
        exposure = (device // NCCD).astype(jnp.int32)
        detector = (device % NCCD).astype(jnp.int32)
        shift_cols = template_shift[exposure, detector].astype(jnp.int32)
        zero_index = jnp.zeros((), jnp.int32)
        window = lax.dynamic_slice(stripe, (exposure, detector * ROWS, shift_cols - margin), (1, ROWS + 2 * margin, COLS + 2 * margin))[0]
        model = convolve(window, kernel_coeff[exposure, detector])
        observed = lax.dynamic_slice(science, (exposure, detector * ROWS, zero_index), (1, ROWS, COLS))[0]
        spread = lax.dynamic_slice(variance, (exposure, detector * ROWS, zero_index), (1, ROWS, COLS))[0]
        snr = (observed - model) / jnp.sqrt(spread)
        stamps = cut_stamps(snr, corner_rows[exposure, detector], corner_cols[exposure, detector])
        objects = (owner_device[exposure, detector, :, 0] * OBJ_DEV + object_slot[exposure, detector]).astype(jnp.int32)
        sums = sums.at[objects].add(stamps.astype(jnp.float32))
        counts = counts.at[objects].add(jnp.ones((objects.shape[0],), jnp.float32))
        return ((sums, counts), device)
    start = (jnp.zeros((OBJECTS, CUT * CUT), jnp.float32), jnp.zeros((OBJECTS,), jnp.float32))
    (sums, counts), visited = lax.scan(visit, start, jnp.arange(DEVS, dtype=jnp.int32))
    return sums / jnp.maximum(counts, 1.0)[:, None]
```

```python
import functools

import jax
import jax.numpy as jnp
import numpy as np
from jax import lax
from jax.experimental import pallas as pl
from jax.experimental.pallas import tpu as pltpu
from jax.sharding import PartitionSpec as P

KW = 21
CUT = 32
OBJ_DEV = 128
HALO = 16
MARGIN = KW // 2
SIGMAS = (1.0, 2.0, 3.5)
POWERS = 4
MESH = pl.DeviceIdType.MESH
LIMIT = 48 * 1024 * 1024


def profiles():
    offsets = np.arange(KW) - MARGIN
    out = np.zeros((len(SIGMAS), POWERS, KW))
    for group, sigma in enumerate(SIGMAS):
        scaled = offsets / sigma
        for power in range(POWERS):
            value = scaled**power * np.exp(-0.5 * scaled * scaled)
            out[group, power] = value / np.sqrt(np.sum(value * value))
    return out


def column_table(span):
    table = np.zeros((2 * span, len(SIGMAS) * POWERS * span), np.float32)
    shapes = profiles().reshape(-1, KW)
    for index, shape in enumerate(shapes):
        for column in range(span):
            table[column : column + KW, index * span + column] = shape
    return table


def row_table(tile_rows):
    height = tile_rows + 2 * HALO
    table = np.zeros((POWERS, tile_rows, len(SIGMAS), POWERS, height), np.float32)
    shapes = profiles().astype(np.float32)
    for power in range(POWERS):
        for row in range(tile_rows):
            first = row + HALO - MARGIN
            table[power, row, :, :, first : first + KW] = shapes[:, power][:, None, :]
    return table.reshape(POWERS, tile_rows, len(SIGMAS) * POWERS * height)


def gather_kernel(
    nexp,
    nccd,
    cap,
    shift_ref,
    science_ref,
    variance_ref,
    template_ref,
    meta_ref,
    coeff_ref,
    cols_ref,
    rows_ref,
    tiles_ref,
    codes_ref,
    stripe,
    metas,
    weights,
    halo_send,
    halo_recv,
    sems,
):
    e = lax.axis_index("exp")
    c = lax.axis_index("ccd")
    count = nexp * nccd
    lanes = nccd // 2
    half = nexp * lanes
    parity = lax.rem(c, 2)
    mine = e * lanes + c // 2
    me = e * nccd + c
    rows = science_ref.shape[0]
    height = rows + 2 * HALO

    barrier = pltpu.get_barrier_semaphore()

    def greet(k, carry):
        other = lax.rem(me + k, count)
        pl.semaphore_signal(
            barrier, inc=1, device_id=(other // nccd, lax.rem(other, nccd)), device_id_type=MESH
        )
        return carry

    lax.fori_loop(1, count, greet, 0)

    metas[parity, mine] = meta_ref[...]
    stripe[0, pl.ds(HALO, rows), :] = template_ref[...]

    @pl.when(c == 0)
    def _():
        stripe[:, pl.ds(0, HALO), :] = jnp.zeros((2, HALO, stripe.shape[2]), jnp.bfloat16)

    @pl.when(c == nccd - 1)
    def _():
        stripe[:, pl.ds(rows + HALO, HALO), :] = jnp.zeros(
            (2, HALO, stripe.shape[2]), jnp.bfloat16
        )

    total = jnp.zeros(rows_ref.shape[1:], jnp.float32)
    for power in range(POWERS):
        total = total + (rows_ref[power] * coeff_ref[pl.ds(power, 1), :]).astype(
            jnp.bfloat16
        ).astype(jnp.float32)
    high = total.astype(jnp.bfloat16)
    weights[pl.ds(0, rows), :] = high
    weights[pl.ds(rows, rows), :] = (total - high.astype(jnp.float32)).astype(jnp.bfloat16)

    pl.semaphore_wait(barrier, count - 1)

    before = lax.rem(e + nexp - 1, nexp)

    def halo(index, src_row, size, side, dst_row, device):
        return pltpu.make_async_remote_copy(
            src_ref=template_ref.at[pl.ds(src_row, size)],
            dst_ref=stripe.at[side, pl.ds(dst_row, size)],
            send_sem=halo_send.at[index],
            recv_sem=halo_recv.at[index],
            device_id=device,
            device_id_type=MESH,
        )

    full = halo(0, 0, rows, 1, HALO, (before, c))
    down = [
        halo(1, rows - HALO, HALO, 0, 0, (e, c + 1)),
        halo(2, rows - HALO, HALO, 1, 0, (before, c + 1)),
    ]
    up = [
        halo(3, 0, HALO, 0, rows + HALO, (e, c - 1)),
        halo(4, 0, HALO, 1, rows + HALO, (before, c - 1)),
    ]
    full.start()

    @pl.when(c < nccd - 1)
    def _():
        for copy in down:
            copy.start()

    @pl.when(c > 0)
    def _():
        for copy in up:
            copy.start()

    def spread(ref, send, recv):
        def body(k, carry):
            other = lax.rem(mine + k, half)
            pltpu.make_async_remote_copy(
                src_ref=ref.at[parity, mine],
                dst_ref=ref.at[parity, mine],
                send_sem=sems.at[send],
                recv_sem=sems.at[recv],
                device_id=(other // lanes, lax.rem(other, lanes) * 2 + parity),
                device_id_type=MESH,
            ).start()
            return carry

        lax.fori_loop(1, half, body, 0)

    def wait_spread(ref, sem):
        part = ref.at[0, pl.ds(0, half - 1)]
        pltpu.make_async_copy(part, part, sems.at[sem]).wait()

    def share(ref, send, recv):
        return pltpu.make_async_remote_copy(
            src_ref=ref.at[parity],
            dst_ref=ref.at[parity],
            send_sem=sems.at[send],
            recv_sem=sems.at[recv],
            device_id=(e, c + 1 - 2 * parity),
            device_id_type=MESH,
        )

    spread(metas, 0, 1)

    span = science_ref.shape[1]
    offset = shift_ref[0, 0] - MARGIN
    source = lax.broadcasted_iota(jnp.int32, (2 * span, 2 * span), 0)
    target = lax.broadcasted_iota(jnp.int32, (2 * span, 2 * span), 1)
    pick = (source == target + offset).astype(jnp.float32).astype(jnp.bfloat16)

    full.wait_recv()

    @pl.when(c > 0)
    def _():
        for copy in down:
            copy.wait_recv()

    @pl.when(c < nccd - 1)
    def _():
        for copy in up:
            copy.wait_recv()

    joined = jnp.concatenate([stripe[0], stripe[1]], axis=1)
    window = jnp.dot(joined, pick, preferred_element_type=jnp.float32).astype(jnp.bfloat16)
    smeared = jnp.dot(window, cols_ref[...], preferred_element_type=jnp.float32).astype(
        jnp.bfloat16
    )
    kinds = len(SIGMAS) * POWERS
    stacked = jnp.concatenate(
        [smeared[:, kind * span : (kind + 1) * span] for kind in range(kinds)], axis=0
    )
    both = jnp.dot(weights[...], stacked, preferred_element_type=jnp.float32)
    model = both[:rows] + both[rows:]
    snr = (science_ref[...] - model) / jnp.sqrt(variance_ref[...])
    tiles_ref[parity, mine] = snr.astype(jnp.bfloat16)
    spread(tiles_ref, 2, 3)

    wait_spread(metas, 1)
    meta_share = share(metas, 4, 5)
    meta_share.start()
    meta_share.wait_recv()

    shape = (count, span)
    lower = lax.broadcasted_iota(jnp.int32, (span, span), 0)
    upper = lax.broadcasted_iota(jnp.int32, (span, span), 1)
    earlier = (lower < upper).astype(jnp.float32).astype(jnp.bfloat16)
    lane = lax.broadcasted_iota(jnp.int32, shape, 1)
    rows_of = meta_ref.shape[0] // 4
    table = metas[...].reshape(count, meta_ref.shape[0], span)
    seen = jnp.zeros((count, 1), jnp.float32)
    parts = []
    for part in range(rows_of):
        match = table[:, part, :] == me
        flags = match.astype(jnp.float32)
        place = seen + jnp.dot(
            flags.astype(jnp.bfloat16), earlier, preferred_element_type=jnp.float32
        )
        seen = seen + jnp.sum(flags, axis=1, keepdims=True)
        code = (
            (table[:, rows_of + part, :] + 1) * 8192
            + table[:, 2 * rows_of + part, :] * 128
            + table[:, 3 * rows_of + part, :]
        ).astype(jnp.float32)
        parts.append((jnp.where(match, place, -1.0), code))
    listing = jnp.where(lane == span - 1, seen, 0.0)
    for entry in range(cap):
        found = sum(jnp.where(place == entry, code, 0.0) for place, code in parts)
        listing = jnp.where(lane == entry, jnp.sum(found, axis=1, keepdims=True), listing)
    codes_ref[...] = listing.astype(jnp.int32)

    wait_spread(tiles_ref, 3)
    tile_share = share(tiles_ref, 6, 7)
    tile_share.start()
    tile_share.wait_recv()

    full.wait_send()

    @pl.when(c < nccd - 1)
    def _():
        for copy in down:
            copy.wait_send()

    @pl.when(c > 0)
    def _():
        for copy in up:
            copy.wait_send()

    wait_spread(metas, 0)
    wait_spread(tiles_ref, 2)
    meta_share.wait_send()
    tile_share.wait_send()


GROUP = 4


def stamp_kernel(codes_ref, tiles_ref, out_ref, wide, sums):
    count, rows, span = tiles_ref.shape
    sums[...] = jnp.zeros(sums.shape, jnp.float32)
    lane = lax.broadcasted_iota(jnp.int32, (CUT, span), 1)

    def one_tile(t, carry):
        base = pl.multiple_of(t * rows, rows)
        wide[pl.ds(base, rows), :] = tiles_ref[t].astype(jnp.float32)

        def some(g, inner):
            cuts = []
            for k in range(GROUP):
                code = codes_ref[t, g * GROUP + k]
                top = (code >> 7) & 63
                left = code & 127
                value = pltpu.roll(wide[pl.ds(base + top, CUT), :], (span - left) & (span - 1), 1)
                cuts.append((code >> 13, jnp.where(lane < CUT, value, 1.0)))
            for slot, value in cuts:
                at = pl.ds(pl.multiple_of(slot * CUT, CUT), CUT)
                sums[at, :] = sums[at, :] + value
            return inner

        lax.fori_loop(0, (codes_ref[t, span - 1] + GROUP - 1) // GROUP, some, 0)
        return carry

    lax.fori_loop(0, count, one_tile, 0)

    fold = span // CUT
    lane8 = lax.broadcasted_iota(jnp.int32, (8, span), 1)

    def finish(block, carry):
        first = (block * 8 + 1) * CUT
        tally = jnp.maximum(sums[pl.ds(first, 8, stride=CUT), :][:, CUT : CUT + 1], 1.0)
        for chunk in range(CUT // fold):
            merged = None
            for k in range(fold):
                row = sums[pl.ds(first + chunk * fold + k, 8, stride=CUT), :]
                if k == 0:
                    merged = row
                else:
                    merged = jnp.where(lane8 >= k * CUT, pltpu.roll(row, k * CUT, 1), merged)
            out_ref[pl.ds(pl.multiple_of(block * 8, 8), 8), pl.ds(chunk * span, span)] = (
                merged / tally
            )
        return carry

    lax.fori_loop(0, OBJ_DEV // 8, finish, 0)


def shards(
    nexp,
    nccd,
    science,
    variance,
    template,
    kernel_coeff,
    template_shift,
    corner_rows,
    corner_cols,
    owner_device,
    object_slot,
):
    rows, span = science.shape[1:]
    sources = object_slot.shape[-1]
    count = nexp * nccd
    half = count // 2
    cap = max(2, (2 * sources + count - 1) // count)
    meta = jnp.concatenate(
        [
            part.reshape(sources // span, span)
            for part in (owner_device, object_slot, corner_rows, corner_cols)
        ],
        axis=0,
    )
    height = rows + 2 * HALO
    kinds = len(SIGMAS) * POWERS
    coeff = kernel_coeff.reshape(-1)
    coeff = jnp.pad(coeff, (0, len(SIGMAS) * POWERS * POWERS - coeff.shape[0]))
    coeff = coeff.reshape(len(SIGMAS), POWERS, POWERS).transpose(1, 0, 2).reshape(POWERS, kinds)
    coeff = jnp.repeat(coeff, height, axis=1)
    cols = jnp.asarray(column_table(span)).astype(jnp.bfloat16)
    downs = jnp.asarray(row_table(rows))
    vmem = pl.BlockSpec(memory_space=pltpu.VMEM)
    smem = pl.BlockSpec(memory_space=pltpu.SMEM)
    tiles, codes = pl.pallas_call(
        functools.partial(gather_kernel, nexp, nccd, cap),
        out_shape=(
            jax.ShapeDtypeStruct((2, half, rows, span), jnp.bfloat16),
            jax.ShapeDtypeStruct((count, span), jnp.int32),
        ),
        in_specs=[smem] + [vmem] * 7,
        out_specs=(vmem, vmem),
        scratch_shapes=[
            pltpu.VMEM((2, height, span), jnp.bfloat16),
            pltpu.VMEM((2, half) + meta.shape, jnp.int32),
            pltpu.VMEM((2 * rows, kinds * height), jnp.bfloat16),
            pltpu.SemaphoreType.DMA((5,)),
            pltpu.SemaphoreType.DMA((5,)),
            pltpu.SemaphoreType.DMA((8,)),
        ],
        compiler_params=pltpu.CompilerParams(
            collective_id=0, has_side_effects=True, vmem_limit_bytes=LIMIT
        ),
        name="snr_gather",
    )(
        template_shift,
        science[0],
        variance[0],
        template[0],
        meta,
        coeff,
        cols,
        downs,
    )
    return pl.pallas_call(
        stamp_kernel,
        out_shape=jax.ShapeDtypeStruct((OBJ_DEV, CUT * CUT), jnp.float32),
        in_specs=[smem, vmem],
        out_specs=vmem,
        scratch_shapes=[
            pltpu.VMEM((count * rows, span), jnp.float32),
            pltpu.VMEM(((OBJ_DEV + 1) * CUT, span), jnp.float32),
        ],
        compiler_params=pltpu.CompilerParams(vmem_limit_bytes=LIMIT),
        name="stamp_sums",
    )(codes, tiles.reshape(count, rows, span))


def solution(mesh):
    placed = (
        P("exp", "ccd", None),
        P("exp", "ccd", None),
        P("exp", "ccd", None),
        P("exp", "ccd", None),
        P("exp", "ccd"),
        P("exp", "ccd", None),
        P("exp", "ccd", None),
        P("exp", "ccd", None, None),
        P("exp", "ccd", None),
    )
    return jax.shard_map(
        functools.partial(shards, mesh.shape["exp"], mesh.shape["ccd"]),
        mesh=mesh,
        in_specs=placed,
        out_specs=P(("exp", "ccd"), None),
        check_vma=False,
    )
```

```python
import functools

import jax
import jax.numpy as jnp
import numpy as np
from jax import lax
from jax.experimental import pallas as pl
from jax.experimental.pallas import tpu as pltpu
from jax.sharding import PartitionSpec as P

KW = 21
CUT = 32
OBJ_DEV = 128
HALO = 16
MARGIN = KW // 2
SIGMAS = (1.0, 2.0, 3.5)
POWERS = 4
MESH = pl.DeviceIdType.MESH
LIMIT = 60 * 1024 * 1024


def profiles():
    offsets = np.arange(KW) - MARGIN
    out = np.zeros((len(SIGMAS), POWERS, KW))
    for group, sigma in enumerate(SIGMAS):
        scaled = offsets / sigma
        for power in range(POWERS):
            value = scaled**power * np.exp(-0.5 * scaled * scaled)
            out[group, power] = value / np.sqrt(np.sum(value * value))
    return out


def column_table(span):
    table = np.zeros((2 * span, len(SIGMAS) * POWERS * span), np.float32)
    shapes = profiles().reshape(-1, KW)
    for index, shape in enumerate(shapes):
        for column in range(span):
            table[column : column + KW, index * span + column] = shape
    return table


def row_table(tile_rows):
    height = tile_rows + 2 * HALO
    table = np.zeros((POWERS, tile_rows, len(SIGMAS), POWERS, height), np.float32)
    shapes = profiles().astype(np.float32)
    for power in range(POWERS):
        for row in range(tile_rows):
            first = row + HALO - MARGIN
            table[power, row, :, :, first : first + KW] = shapes[:, power][:, None, :]
    return table.reshape(POWERS, tile_rows, len(SIGMAS) * POWERS * height)


def gather_kernel(
    nexp,
    nccd,
    cap,
    shift_ref,
    science_hbm,
    variance_hbm,
    template_hbm,
    owner_hbm,
    slot_hbm,
    top_hbm,
    left_hbm,
    coeff_hbm,
    cols_hbm,
    rows_hbm,
    tiles_ref,
    codes_ref,
    science_ref,
    variance_ref,
    coeff_ref,
    cols_ref,
    rows_ref,
    stripe,
    metas,
    weights,
    load_sems,
    halo_send,
    halo_recv,
    sems,
):
    e = lax.axis_index("exp")
    c = lax.axis_index("ccd")
    count = nexp * nccd
    lanes = nccd // 2
    half = nexp * lanes
    parity = lax.rem(c, 2)
    mine = e * lanes + c // 2
    me = e * nccd + c
    rows = science_ref.shape[0]
    height = rows + 2 * HALO

    fields = (owner_hbm, slot_hbm, top_hbm, left_hbm)
    rows_of = owner_hbm.shape[0]
    pairs = [(template_hbm, stripe.at[0, pl.ds(HALO, rows)])]
    for index, field in enumerate(fields):
        pairs.append((field, metas.at[parity, mine, pl.ds(index * rows_of, rows_of)]))
    pairs += [
        (coeff_hbm, coeff_ref),
        (rows_hbm, rows_ref),
        (cols_hbm, cols_ref),
        (science_hbm, science_ref),
        (variance_hbm, variance_ref),
    ]
    loads = [
        pltpu.make_async_copy(source, target, load_sems.at[index])
        for index, (source, target) in enumerate(pairs)
    ]
    for load in loads:
        load.start()

    barrier = pltpu.get_barrier_semaphore()

    def greet(k, carry):
        other = lax.rem(me + k, count)
        pl.semaphore_signal(
            barrier, inc=1, device_id=(other // nccd, lax.rem(other, nccd)), device_id_type=MESH
        )
        return carry

    lax.fori_loop(1, count, greet, 0)

    @pl.when(c == 0)
    def _():
        stripe[:, pl.ds(0, HALO), :] = jnp.zeros((2, HALO, stripe.shape[2]), jnp.bfloat16)

    @pl.when(c == nccd - 1)
    def _():
        stripe[:, pl.ds(rows + HALO, HALO), :] = jnp.zeros(
            (2, HALO, stripe.shape[2]), jnp.bfloat16
        )

    for load in loads[:5]:
        load.wait()
    pl.semaphore_wait(barrier, count - 1)

    before = lax.rem(e + nexp - 1, nexp)

    def halo(index, src_row, size, side, dst_row, device):
        return pltpu.make_async_remote_copy(
            src_ref=stripe.at[0, pl.ds(HALO + src_row, size)],
            dst_ref=stripe.at[side, pl.ds(dst_row, size)],
            send_sem=halo_send.at[index],
            recv_sem=halo_recv.at[index],
            device_id=device,
            device_id_type=MESH,
        )

    full = halo(0, 0, rows, 1, HALO, (before, c))
    down = [
        halo(1, rows - HALO, HALO, 0, 0, (e, c + 1)),
        halo(2, rows - HALO, HALO, 1, 0, (before, c + 1)),
    ]
    up = [
        halo(3, 0, HALO, 0, rows + HALO, (e, c - 1)),
        halo(4, 0, HALO, 1, rows + HALO, (before, c - 1)),
    ]
    full.start()

    @pl.when(c < nccd - 1)
    def _():
        for copy in down:
            copy.start()

    @pl.when(c > 0)
    def _():
        for copy in up:
            copy.start()

    def spread(ref, send, recv):
        def body(k, carry):
            other = lax.rem(mine + k, half)
            pltpu.make_async_remote_copy(
                src_ref=ref.at[parity, mine],
                dst_ref=ref.at[parity, mine],
                send_sem=sems.at[send],
                recv_sem=sems.at[recv],
                device_id=(other // lanes, lax.rem(other, lanes) * 2 + parity),
                device_id_type=MESH,
            ).start()
            return carry

        lax.fori_loop(1, half, body, 0)

    def wait_spread(ref, sem):
        part = ref.at[0, pl.ds(0, half - 1)]
        pltpu.make_async_copy(part, part, sems.at[sem]).wait()

    def share(ref, send, recv):
        return pltpu.make_async_remote_copy(
            src_ref=ref.at[parity],
            dst_ref=ref.at[parity],
            send_sem=sems.at[send],
            recv_sem=sems.at[recv],
            device_id=(e, c + 1 - 2 * parity),
            device_id_type=MESH,
        )

    spread(metas, 0, 1)

    span = science_ref.shape[1]
    offset = shift_ref[0, 0] - MARGIN
    source = lax.broadcasted_iota(jnp.int32, (2 * span, 2 * span), 0)
    target = lax.broadcasted_iota(jnp.int32, (2 * span, 2 * span), 1)
    pick = (source == target + offset).astype(jnp.float32).astype(jnp.bfloat16)

    for load in loads[5:7]:
        load.wait()
    wide = rows_ref.shape[2]
    bases = coeff_ref.shape[1]
    basis = lax.broadcasted_iota(jnp.int32, (8, bases), 1)
    which = lax.broadcasted_iota(jnp.int32, (8, bases), 0)
    split = jnp.where((basis // POWERS) % POWERS == which, coeff_ref[...], 0.0)
    basis = lax.broadcasted_iota(jnp.int32, (bases, wide), 0)
    kind = lax.broadcasted_iota(jnp.int32, (bases, wide), 1) // height
    owns = (basis // (POWERS * POWERS)) * POWERS + basis % POWERS == kind
    spread_coeff = jnp.dot(
        split,
        owns.astype(jnp.float32),
        precision=lax.Precision.HIGHEST,
        preferred_element_type=jnp.float32,
    )
    total = jnp.zeros(rows_ref.shape[1:], jnp.float32)
    for power in range(POWERS):
        total = total + (rows_ref[power] * spread_coeff[power : power + 1]).astype(
            jnp.bfloat16
        ).astype(jnp.float32)
    high = total.astype(jnp.bfloat16)
    weights[pl.ds(0, rows), :] = high
    weights[pl.ds(rows, rows), :] = (total - high.astype(jnp.float32)).astype(jnp.bfloat16)

    for load in loads[7:]:
        load.wait()

    full.wait_recv()

    @pl.when(c > 0)
    def _():
        for copy in down:
            copy.wait_recv()

    @pl.when(c < nccd - 1)
    def _():
        for copy in up:
            copy.wait_recv()

    joined = jnp.concatenate([stripe[0], stripe[1]], axis=1)
    window = jnp.dot(joined, pick, preferred_element_type=jnp.float32).astype(jnp.bfloat16)
    smeared = jnp.dot(window, cols_ref[...], preferred_element_type=jnp.float32).astype(
        jnp.bfloat16
    )
    kinds = len(SIGMAS) * POWERS
    stacked = jnp.concatenate(
        [smeared[:, kind * span : (kind + 1) * span] for kind in range(kinds)], axis=0
    )
    both = jnp.dot(weights[...], stacked, preferred_element_type=jnp.float32)
    model = both[:rows] + both[rows:]
    snr = (science_ref[...] - model) / jnp.sqrt(variance_ref[...])
    tiles_ref[parity, mine] = snr.astype(jnp.bfloat16)
    spread(tiles_ref, 2, 3)

    wait_spread(metas, 1)
    meta_share = share(metas, 4, 5)
    meta_share.start()
    meta_share.wait_recv()

    shape = (count, span)
    lower = lax.broadcasted_iota(jnp.int32, (span, span), 0)
    upper = lax.broadcasted_iota(jnp.int32, (span, span), 1)
    earlier = (lower < upper).astype(jnp.float32).astype(jnp.bfloat16)
    table = metas[...].reshape(count, metas.shape[2], span)
    seen = jnp.zeros((count, 1), jnp.float32)
    parts = []
    for part in range(rows_of):
        match = table[:, part, :] == me
        flags = match.astype(jnp.float32)
        place = seen + jnp.dot(
            flags.astype(jnp.bfloat16), earlier, preferred_element_type=jnp.float32
        )
        seen = seen + jnp.sum(flags, axis=1, keepdims=True)
        code = (
            (table[:, rows_of + part, :] + 1) * 8192
            + table[:, 2 * rows_of + part, :] * 128
            + table[:, 3 * rows_of + part, :]
        ).astype(jnp.float32)
        parts.append((jnp.where(match, place, -1.0), code))
    length = codes_ref.shape[1]
    tri = lax.broadcasted_iota(jnp.int32, (count, count), 1) < lax.broadcasted_iota(
        jnp.int32, (count, count), 0
    )
    starts = jnp.dot(
        tri.astype(jnp.float32).astype(jnp.bfloat16),
        jnp.broadcast_to(seen, shape).astype(jnp.bfloat16),
        preferred_element_type=jnp.float32,
    )[:, :1].astype(jnp.int32)
    ends = starts + seen.astype(jnp.int32)
    tile_row = lax.broadcasted_iota(jnp.int32, (count, 1), 0) * rows
    ahead = lax.broadcasted_iota(jnp.int32, (count, length), 1)
    ahead = jnp.where(ahead < ends, ahead - starts, -1)
    listing = jnp.zeros((count, length), jnp.int32)
    for entry in range(cap):
        found = sum(jnp.where(place == entry, code, 0.0) for place, code in parts)
        code = jnp.sum(found, axis=1, keepdims=True).astype(jnp.int32)
        code = (code >> 13) * 4194304 + (((code >> 7) & 63) + tile_row) * 128 + (code & 127)
        listing = jnp.where(ahead == entry, code, listing)
    codes_ref[...] = jnp.concatenate(
        [
            jnp.sum(listing, axis=0, keepdims=True),
            jnp.broadcast_to(jnp.sum(seen.astype(jnp.int32), axis=0, keepdims=True), (1, length)),
        ],
        axis=0,
    )

    wait_spread(tiles_ref, 3)
    tile_share = share(tiles_ref, 6, 7)
    tile_share.start()
    tile_share.wait_recv()

    full.wait_send()

    @pl.when(c < nccd - 1)
    def _():
        for copy in down:
            copy.wait_send()

    @pl.when(c > 0)
    def _():
        for copy in up:
            copy.wait_send()

    wait_spread(metas, 0)
    wait_spread(tiles_ref, 2)
    meta_share.wait_send()
    tile_share.wait_send()


GROUP = 8


def stamp_kernel(codes_ref, tiles_ref, out_ref, wide, even, odd):
    count, rows, span = tiles_ref.shape
    sums = (even, odd)
    chunk_tiles = 4

    def widen(step, carry):
        for k in range(chunk_tiles):
            t = step * chunk_tiles + k
            wide[pl.ds(pl.multiple_of(t * rows, rows), rows), :] = tiles_ref[t].astype(
                jnp.float32
            )
        return carry

    lax.fori_loop(0, count // chunk_tiles, widen, 0)

    def clear(step, carry):
        at = pl.ds(pl.multiple_of(step * CUT * 4, CUT * 4), CUT * 4)
        for part in sums:
            part[at, :] = jnp.zeros((CUT * 4, span), jnp.float32)
        return carry

    lax.fori_loop(0, even.shape[0] // (CUT * 4), clear, 0)
    lane = lax.broadcasted_iota(jnp.int32, (CUT, span), 1)

    def some(g, carry):
        cuts = []
        for k in range(GROUP):
            code = codes_ref[0, g * GROUP + k]
            value = pltpu.roll(
                wide[pl.ds((code >> 7) & 32767, CUT), :], (span - (code & 127)) & (span - 1), 1
            )
            cuts.append((code >> 22, jnp.where(lane < CUT, value, 1.0)))
        for k, (slot, value) in enumerate(cuts):
            at = pl.ds(pl.multiple_of(slot * CUT, CUT), CUT)
            sums[k % 2][at, :] = sums[k % 2][at, :] + value
        return carry

    lax.fori_loop(0, (codes_ref[1, 0] + GROUP - 1) // GROUP, some, 0)

    fold = span // CUT
    lane8 = lax.broadcasted_iota(jnp.int32, (8, span), 1)

    def finish(block, carry):
        first = (block * 8 + 1) * CUT

        def at_row(row):
            rows8 = pl.ds(first + row, 8, stride=CUT)
            return even[rows8, :] + odd[rows8, :]

        tally = jnp.maximum(at_row(0)[:, CUT : CUT + 1], 1.0)
        for chunk in range(CUT // fold):
            merged = None
            for k in range(fold):
                row = at_row(chunk * fold + k)
                if k == 0:
                    merged = row
                else:
                    merged = jnp.where(lane8 >= k * CUT, pltpu.roll(row, k * CUT, 1), merged)
            out_ref[pl.ds(pl.multiple_of(block * 8, 8), 8), pl.ds(chunk * span, span)] = (
                merged / tally
            )
        return carry

    lax.fori_loop(0, OBJ_DEV // 8, finish, 0)


def shards(
    nexp,
    nccd,
    science,
    variance,
    template,
    kernel_coeff,
    template_shift,
    corner_rows,
    corner_cols,
    owner_device,
    object_slot,
):
    rows, span = science.shape[1:]
    sources = object_slot.shape[-1]
    count = nexp * nccd
    half = count // 2
    cap = max(2, (2 * sources + count - 1) // count)
    fields = [
        part.reshape(sources // span, span)
        for part in (owner_device, object_slot, corner_rows, corner_cols)
    ]
    meta_shape = (4 * (sources // span), span)
    length = count * cap
    height = rows + 2 * HALO
    kinds = len(SIGMAS) * POWERS
    cols = jnp.asarray(column_table(span)).astype(jnp.bfloat16)
    downs = jnp.asarray(row_table(rows))
    vmem = pl.BlockSpec(memory_space=pltpu.VMEM)
    smem = pl.BlockSpec(memory_space=pltpu.SMEM)
    tiles, codes = pl.pallas_call(
        functools.partial(gather_kernel, nexp, nccd, cap),
        out_shape=(
            jax.ShapeDtypeStruct((2, half, rows, span), jnp.bfloat16),
            jax.ShapeDtypeStruct((2, length), jnp.int32),
        ),
        in_specs=[smem] + [pl.BlockSpec(memory_space=pl.ANY)] * 10,
        out_specs=(vmem, vmem),
        scratch_shapes=[
            pltpu.VMEM((rows, span), jnp.float32),
            pltpu.VMEM((rows, span), jnp.float32),
            pltpu.VMEM(kernel_coeff.shape[1:], jnp.float32),
            pltpu.VMEM(cols.shape, jnp.bfloat16),
            pltpu.VMEM(downs.shape, jnp.float32),
            pltpu.VMEM((2, height, span), jnp.bfloat16),
            pltpu.VMEM((2, half) + meta_shape, jnp.int32),
            pltpu.VMEM((2 * rows, kinds * height), jnp.bfloat16),
            pltpu.SemaphoreType.DMA((10,)),
            pltpu.SemaphoreType.DMA((5,)),
            pltpu.SemaphoreType.DMA((5,)),
            pltpu.SemaphoreType.DMA((8,)),
        ],
        compiler_params=pltpu.CompilerParams(
            collective_id=0, has_side_effects=True, vmem_limit_bytes=LIMIT
        ),
        name="snr_gather",
    )(
        template_shift,
        science[0],
        variance[0],
        template[0],
        *fields,
        kernel_coeff[0],
        cols,
        downs,
    )
    return pl.pallas_call(
        stamp_kernel,
        out_shape=jax.ShapeDtypeStruct((OBJ_DEV, CUT * CUT), jnp.float32),
        in_specs=[smem, vmem],
        out_specs=vmem,
        scratch_shapes=[
            pltpu.VMEM((count * rows, span), jnp.float32),
            pltpu.VMEM(((OBJ_DEV + 4) * CUT, span), jnp.float32),
            pltpu.VMEM(((OBJ_DEV + 4) * CUT, span), jnp.float32),
        ],
        compiler_params=pltpu.CompilerParams(vmem_limit_bytes=LIMIT),
        name="stamp_sums",
    )(codes, tiles.reshape(count, rows, span))


def solution(mesh):
    placed = (
        P("exp", "ccd", None),
        P("exp", "ccd", None),
        P("exp", "ccd", None),
        P("exp", "ccd", None),
        P("exp", "ccd"),
        P("exp", "ccd", None),
        P("exp", "ccd", None),
        P("exp", "ccd", None, None),
        P("exp", "ccd", None),
    )
    return jax.shard_map(
        functools.partial(shards, mesh.shape["exp"], mesh.shape["ccd"]),
        mesh=mesh,
        in_specs=placed,
        out_specs=P(("exp", "ccd"), None),
        check_vma=False,
    )
```

```python
import functools

import jax
import jax.numpy as jnp
import numpy as np
from jax import lax
from jax.experimental import pallas as pl
from jax.experimental.pallas import tpu as pltpu
from jax.sharding import PartitionSpec as P

KW = 21
CUT = 32
OBJ_DEV = 128
HALO = 16
MARGIN = KW // 2
SIGMAS = (1.0, 2.0, 3.5)
POWERS = 4
MESH = pl.DeviceIdType.MESH
LIMIT = 60 * 1024 * 1024


def profiles():
    offsets = np.arange(KW) - MARGIN
    out = np.zeros((len(SIGMAS), POWERS, KW))
    for group, sigma in enumerate(SIGMAS):
        scaled = offsets / sigma
        for power in range(POWERS):
            value = scaled**power * np.exp(-0.5 * scaled * scaled)
            out[group, power] = value / np.sqrt(np.sum(value * value))
    return out


def column_table(span):
    table = np.zeros((2 * span, len(SIGMAS) * POWERS * span), np.float32)
    shapes = profiles().reshape(-1, KW)
    for index, shape in enumerate(shapes):
        for column in range(span):
            table[column : column + KW, index * span + column] = shape
    return table


def row_table(tile_rows):
    height = tile_rows + 2 * HALO
    table = np.zeros((POWERS, tile_rows, len(SIGMAS), POWERS, height), np.float32)
    shapes = profiles().astype(np.float32)
    for power in range(POWERS):
        for row in range(tile_rows):
            first = row + HALO - MARGIN
            table[power, row, :, :, first : first + KW] = shapes[:, power][:, None, :]
    return table.reshape(POWERS, tile_rows, len(SIGMAS) * POWERS * height)


def gather_kernel(
    nexp,
    nccd,
    cap,
    shift_ref,
    science_hbm,
    variance_hbm,
    template_hbm,
    owner_hbm,
    slot_hbm,
    top_hbm,
    left_hbm,
    coeff_hbm,
    cols_hbm,
    rows_hbm,
    tiles_ref,
    codes_ref,
    tally_ref,
    science_ref,
    variance_ref,
    coeff_ref,
    cols_ref,
    rows_ref,
    stripe,
    metas,
    weights,
    load_sems,
    halo_send,
    halo_recv,
    sems,
):
    e = lax.axis_index("exp")
    c = lax.axis_index("ccd")
    count = nexp * nccd
    lanes = nccd // 2
    half = nexp * lanes
    parity = lax.rem(c, 2)
    mine = e * lanes + c // 2
    me = e * nccd + c
    rows = science_ref.shape[0]
    height = rows + 2 * HALO

    fields = (owner_hbm, slot_hbm, top_hbm, left_hbm)
    rows_of = owner_hbm.shape[0]
    pairs = [(template_hbm, stripe.at[0, pl.ds(HALO, rows)])]
    for index, field in enumerate(fields):
        pairs.append((field, metas.at[parity, mine, pl.ds(index * rows_of, rows_of)]))
    pairs += [
        (coeff_hbm, coeff_ref),
        (rows_hbm, rows_ref),
        (cols_hbm, cols_ref),
        (science_hbm, science_ref),
        (variance_hbm, variance_ref),
    ]
    loads = [
        pltpu.make_async_copy(source, target, load_sems.at[index])
        for index, (source, target) in enumerate(pairs)
    ]
    for load in loads:
        load.start()

    barrier = pltpu.get_barrier_semaphore()

    def greet(k, carry):
        other = lax.rem(me + k, count)
        pl.semaphore_signal(
            barrier, inc=1, device_id=(other // nccd, lax.rem(other, nccd)), device_id_type=MESH
        )
        return carry

    lax.fori_loop(1, count, greet, 0)

    @pl.when(c == 0)
    def _():
        stripe[:, pl.ds(0, HALO), :] = jnp.zeros((2, HALO, stripe.shape[2]), jnp.bfloat16)

    @pl.when(c == nccd - 1)
    def _():
        stripe[:, pl.ds(rows + HALO, HALO), :] = jnp.zeros(
            (2, HALO, stripe.shape[2]), jnp.bfloat16
        )

    for load in loads[:5]:
        load.wait()
    pl.semaphore_wait(barrier, count - 1)

    before = lax.rem(e + nexp - 1, nexp)

    def halo(index, src_row, size, side, dst_row, device):
        return pltpu.make_async_remote_copy(
            src_ref=stripe.at[0, pl.ds(HALO + src_row, size)],
            dst_ref=stripe.at[side, pl.ds(dst_row, size)],
            send_sem=halo_send.at[index],
            recv_sem=halo_recv.at[index],
            device_id=device,
            device_id_type=MESH,
        )

    full = halo(0, 0, rows, 1, HALO, (before, c))
    down = [
        halo(1, rows - HALO, HALO, 0, 0, (e, c + 1)),
        halo(2, rows - HALO, HALO, 1, 0, (before, c + 1)),
    ]
    up = [
        halo(3, 0, HALO, 0, rows + HALO, (e, c - 1)),
        halo(4, 0, HALO, 1, rows + HALO, (before, c - 1)),
    ]
    full.start()

    @pl.when(c < nccd - 1)
    def _():
        for copy in down:
            copy.start()

    @pl.when(c > 0)
    def _():
        for copy in up:
            copy.start()

    def spread(ref, send, recv):
        def body(k, carry):
            other = lax.rem(mine + k, half)
            pltpu.make_async_remote_copy(
                src_ref=ref.at[parity, mine],
                dst_ref=ref.at[parity, mine],
                send_sem=sems.at[send],
                recv_sem=sems.at[recv],
                device_id=(other // lanes, lax.rem(other, lanes) * 2 + parity),
                device_id_type=MESH,
            ).start()
            return carry

        lax.fori_loop(1, half, body, 0)

    def wait_spread(ref, sem):
        part = ref.at[0, pl.ds(0, half - 1)]
        pltpu.make_async_copy(part, part, sems.at[sem]).wait()

    def share(ref, send, recv):
        return pltpu.make_async_remote_copy(
            src_ref=ref.at[parity],
            dst_ref=ref.at[parity],
            send_sem=sems.at[send],
            recv_sem=sems.at[recv],
            device_id=(e, c + 1 - 2 * parity),
            device_id_type=MESH,
        )

    spread(metas, 0, 1)

    span = science_ref.shape[1]
    offset = shift_ref[0, 0] - MARGIN
    source = lax.broadcasted_iota(jnp.int32, (2 * span, 2 * span), 0)
    target = lax.broadcasted_iota(jnp.int32, (2 * span, 2 * span), 1)
    pick = (source == target + offset).astype(jnp.float32).astype(jnp.bfloat16)

    for load in loads[5:7]:
        load.wait()
    wide = rows_ref.shape[2]
    bases = coeff_ref.shape[1]
    basis = lax.broadcasted_iota(jnp.int32, (8, bases), 1)
    which = lax.broadcasted_iota(jnp.int32, (8, bases), 0)
    split = jnp.where((basis // POWERS) % POWERS == which, coeff_ref[...], 0.0)
    basis = lax.broadcasted_iota(jnp.int32, (bases, wide), 0)
    kind = lax.broadcasted_iota(jnp.int32, (bases, wide), 1) // height
    owns = (basis // (POWERS * POWERS)) * POWERS + basis % POWERS == kind
    spread_coeff = jnp.dot(
        split,
        owns.astype(jnp.float32),
        precision=lax.Precision.HIGHEST,
        preferred_element_type=jnp.float32,
    )
    total = jnp.zeros(rows_ref.shape[1:], jnp.float32)
    for power in range(POWERS):
        total = total + (rows_ref[power] * spread_coeff[power : power + 1]).astype(
            jnp.bfloat16
        ).astype(jnp.float32)
    high = total.astype(jnp.bfloat16)
    weights[pl.ds(0, rows), :] = high
    weights[pl.ds(rows, rows), :] = (total - high.astype(jnp.float32)).astype(jnp.bfloat16)

    for load in loads[7:]:
        load.wait()

    full.wait_recv()

    @pl.when(c > 0)
    def _():
        for copy in down:
            copy.wait_recv()

    @pl.when(c < nccd - 1)
    def _():
        for copy in up:
            copy.wait_recv()

    joined = jnp.concatenate([stripe[0], stripe[1]], axis=1)
    window = jnp.dot(joined, pick, preferred_element_type=jnp.float32).astype(jnp.bfloat16)
    smeared = jnp.dot(window, cols_ref[...], preferred_element_type=jnp.float32).astype(
        jnp.bfloat16
    )
    kinds = len(SIGMAS) * POWERS
    stacked = jnp.concatenate(
        [smeared[:, kind * span : (kind + 1) * span] for kind in range(kinds)], axis=0
    )
    both = jnp.dot(weights[...], stacked, preferred_element_type=jnp.float32)
    model = both[:rows] + both[rows:]
    snr = (science_ref[...] - model) / jnp.sqrt(variance_ref[...])
    tiles_ref[parity, mine] = snr.astype(jnp.bfloat16)
    spread(tiles_ref, 2, 3)

    wait_spread(metas, 1)
    meta_share = share(metas, 4, 5)
    meta_share.start()
    meta_share.wait_recv()

    shape = (count, span)
    lower = lax.broadcasted_iota(jnp.int32, (span, span), 0)
    upper = lax.broadcasted_iota(jnp.int32, (span, span), 1)
    earlier = (lower < upper).astype(jnp.float32).astype(jnp.bfloat16)
    table = metas[...].reshape(count, metas.shape[2], span)
    seen = jnp.zeros((count, 1), jnp.float32)
    parts = []
    for part in range(rows_of):
        match = table[:, part, :] == me
        flags = match.astype(jnp.float32)
        place = seen + jnp.dot(
            flags.astype(jnp.bfloat16), earlier, preferred_element_type=jnp.float32
        )
        seen = seen + jnp.sum(flags, axis=1, keepdims=True)
        code = (
            (table[:, rows_of + part, :] + 1) * 8192
            + table[:, 2 * rows_of + part, :] * 128
            + table[:, 3 * rows_of + part, :]
        ).astype(jnp.float32)
        parts.append((jnp.where(match, place, -1.0), code))
    length = codes_ref.shape[1]
    tri = lax.broadcasted_iota(jnp.int32, (count, count), 1) < lax.broadcasted_iota(
        jnp.int32, (count, count), 0
    )
    starts = jnp.dot(
        tri.astype(jnp.float32).astype(jnp.bfloat16),
        jnp.broadcast_to(seen, shape).astype(jnp.bfloat16),
        preferred_element_type=jnp.float32,
    )[:, :1].astype(jnp.int32)
    ends = starts + seen.astype(jnp.int32)
    tile_row = lax.broadcasted_iota(jnp.int32, (count, 1), 0) * rows
    ahead = lax.broadcasted_iota(jnp.int32, (count, length), 1)
    ahead = jnp.where(ahead < ends, ahead - starts, -1)
    listing = jnp.zeros((count, length), jnp.int32)
    for entry in range(cap):
        found = sum(jnp.where(place == entry, code, 0.0) for place, code in parts)
        code = jnp.sum(found, axis=1, keepdims=True).astype(jnp.int32)
        code = (code >> 13) * 4194304 + (((code >> 7) & 63) + tile_row) * 128 + (code & 127)
        listing = jnp.where(ahead == entry, code, listing)
    listing = jnp.sum(listing, axis=0, keepdims=True)
    slots = lax.broadcasted_iota(jnp.int32, (OBJ_DEV, length), 0) + 1
    tally = jnp.sum((slots == (listing >> 22)).astype(jnp.float32), axis=1, keepdims=True)
    tally_ref[...] = jnp.broadcast_to(jnp.maximum(tally, 1.0), tally_ref.shape)
    codes_ref[...] = jnp.concatenate(
        [
            listing,
            jnp.broadcast_to(jnp.sum(seen.astype(jnp.int32), axis=0, keepdims=True), (1, length)),
        ],
        axis=0,
    )

    wait_spread(tiles_ref, 3)
    tile_share = share(tiles_ref, 6, 7)
    tile_share.start()
    tile_share.wait_recv()

    full.wait_send()

    @pl.when(c < nccd - 1)
    def _():
        for copy in down:
            copy.wait_send()

    @pl.when(c > 0)
    def _():
        for copy in up:
            copy.wait_send()

    wait_spread(metas, 0)
    wait_spread(tiles_ref, 2)
    meta_share.wait_send()
    tile_share.wait_send()


GROUP = 16
PARTS = 4
PACK = 8


def stamp_kernel(codes_ref, tiles_ref, tally_ref, out_ref, wide, *sums):
    count, rows, span = tiles_ref.shape
    fold = span // CUT
    chunk_tiles = 4

    def widen(step, carry):
        for k in range(chunk_tiles):
            t = step * chunk_tiles + k
            wide[pl.ds(pl.multiple_of(t * rows, rows), rows), :] = tiles_ref[t].astype(
                jnp.float32
            )
        return carry

    lax.fori_loop(0, count // chunk_tiles, widen, 0)
    for part in sums:
        part[...] = jnp.zeros(part.shape, jnp.float32)
    lane = lax.broadcasted_iota(jnp.int32, (PACK, span), 1)

    def some(g, carry):
        cuts = []
        for k in range(GROUP):
            code = codes_ref[0, g * GROUP + k]
            top = (code >> 7) & 32767
            packed = None
            for q in range(fold):
                value = pltpu.roll(
                    wide[pl.ds(top + q * PACK, PACK), :],
                    (span + q * CUT - (code & 127)) & (span - 1),
                    1,
                )
                packed = value if q == 0 else jnp.where(lane >= q * CUT, value, packed)
            cuts.append((code >> 22, packed))
        for k, (slot, value) in enumerate(cuts):
            at = pl.ds(pl.multiple_of(slot * PACK, PACK), PACK)
            sums[k % PARTS][at, :] = sums[k % PARTS][at, :] + value
        return carry

    lax.fori_loop(0, (codes_ref[1, 0] + GROUP - 1) // GROUP, some, 0)
    sums[0][...] = (sums[0][...] + sums[1][...]) + (sums[2][...] + sums[3][...])

    def finish(block, carry):
        first = (block * 8 + 1) * PACK
        slots = pl.ds(pl.multiple_of(block * 8, 8), 8)
        tally = tally_ref[slots, :]
        lines = [sums[0][pl.ds(first + r, 8, stride=PACK), :] for r in range(PACK)]
        for q in range(fold):
            for h in range(PACK // fold):
                merged = None
                for k in range(fold):
                    line = lines[h * fold + k]
                    turn = ((k - q) * CUT) % span
                    line = pltpu.roll(line, turn, 1) if turn else line
                    merged = line if k == 0 else jnp.where(lane >= k * CUT, line, merged)
                chunk = q * (PACK // fold) + h
                out_ref[slots, pl.ds(chunk * span, span)] = merged / tally
        return carry

    lax.fori_loop(0, OBJ_DEV // 8, finish, 0)


def shards(
    nexp,
    nccd,
    science,
    variance,
    template,
    kernel_coeff,
    template_shift,
    corner_rows,
    corner_cols,
    owner_device,
    object_slot,
):
    rows, span = science.shape[1:]
    sources = object_slot.shape[-1]
    count = nexp * nccd
    half = count // 2
    cap = max(2, (2 * sources + count - 1) // count)
    fields = [
        part.reshape(sources // span, span)
        for part in (owner_device, object_slot, corner_rows, corner_cols)
    ]
    meta_shape = (4 * (sources // span), span)
    length = count * cap
    height = rows + 2 * HALO
    kinds = len(SIGMAS) * POWERS
    cols = jnp.asarray(column_table(span)).astype(jnp.bfloat16)
    downs = jnp.asarray(row_table(rows))
    vmem = pl.BlockSpec(memory_space=pltpu.VMEM)
    smem = pl.BlockSpec(memory_space=pltpu.SMEM)
    tiles, codes, tally = pl.pallas_call(
        functools.partial(gather_kernel, nexp, nccd, cap),
        out_shape=(
            jax.ShapeDtypeStruct((2, half, rows, span), jnp.bfloat16),
            jax.ShapeDtypeStruct((2, length), jnp.int32),
            jax.ShapeDtypeStruct((OBJ_DEV, span), jnp.float32),
        ),
        in_specs=[smem] + [pl.BlockSpec(memory_space=pl.ANY)] * 10,
        out_specs=(vmem, vmem, vmem),
        scratch_shapes=[
            pltpu.VMEM((rows, span), jnp.float32),
            pltpu.VMEM((rows, span), jnp.float32),
            pltpu.VMEM(kernel_coeff.shape[1:], jnp.float32),
            pltpu.VMEM(cols.shape, jnp.bfloat16),
            pltpu.VMEM(downs.shape, jnp.float32),
            pltpu.VMEM((2, height, span), jnp.bfloat16),
            pltpu.VMEM((2, half) + meta_shape, jnp.int32),
            pltpu.VMEM((2 * rows, kinds * height), jnp.bfloat16),
            pltpu.SemaphoreType.DMA((10,)),
            pltpu.SemaphoreType.DMA((5,)),
            pltpu.SemaphoreType.DMA((5,)),
            pltpu.SemaphoreType.DMA((8,)),
        ],
        compiler_params=pltpu.CompilerParams(
            collective_id=0, has_side_effects=True, vmem_limit_bytes=LIMIT
        ),
        name="snr_gather",
    )(
        template_shift,
        science[0],
        variance[0],
        template[0],
        *fields,
        kernel_coeff[0],
        cols,
        downs,
    )
    return pl.pallas_call(
        stamp_kernel,
        out_shape=jax.ShapeDtypeStruct((OBJ_DEV, CUT * CUT), jnp.float32),
        in_specs=[smem, vmem, vmem],
        out_specs=vmem,
        scratch_shapes=[
            pltpu.VMEM((count * rows, span), jnp.float32),
        ]
        + [pltpu.VMEM(((OBJ_DEV + 1) * PACK, span), jnp.float32)] * PARTS,
        compiler_params=pltpu.CompilerParams(vmem_limit_bytes=LIMIT),
        name="stamp_sums",
    )(codes, tiles.reshape(count, rows, span), tally)


def solution(mesh):
    placed = (
        P("exp", "ccd", None),
        P("exp", "ccd", None),
        P("exp", "ccd", None),
        P("exp", "ccd", None),
        P("exp", "ccd"),
        P("exp", "ccd", None),
        P("exp", "ccd", None),
        P("exp", "ccd", None, None),
        P("exp", "ccd", None),
    )
    return jax.shard_map(
        functools.partial(shards, mesh.shape["exp"], mesh.shape["ccd"]),
        mesh=mesh,
        in_specs=placed,
        out_specs=P(("exp", "ccd"), None),
        check_vma=False,
    )
```

```python
import functools

import jax
import jax.numpy as jnp
import numpy as np
from jax import lax
from jax.experimental import pallas as pl
from jax.experimental.pallas import tpu as pltpu
from jax.sharding import PartitionSpec as P

KW = 21
CUT = 32
OBJ_DEV = 128
HALO = 16
MARGIN = KW // 2
SIGMAS = (1.0, 2.0, 3.5)
POWERS = 4
MESH = pl.DeviceIdType.MESH
LIMIT = 60 * 1024 * 1024


def profiles():
    offsets = np.arange(KW) - MARGIN
    out = np.zeros((len(SIGMAS), POWERS, KW))
    for group, sigma in enumerate(SIGMAS):
        scaled = offsets / sigma
        for power in range(POWERS):
            value = scaled**power * np.exp(-0.5 * scaled * scaled)
            out[group, power] = value / np.sqrt(np.sum(value * value))
    return out


def column_table(span):
    table = np.zeros((2 * span, len(SIGMAS) * POWERS * span), np.float32)
    shapes = profiles().reshape(-1, KW)
    for index, shape in enumerate(shapes):
        for column in range(span):
            table[column : column + KW, index * span + column] = shape
    return table


def row_table(tile_rows):
    height = tile_rows + 2 * HALO
    table = np.zeros((POWERS, tile_rows, len(SIGMAS), POWERS, height), np.float32)
    shapes = profiles().astype(np.float32)
    for power in range(POWERS):
        for row in range(tile_rows):
            first = row + HALO - MARGIN
            table[power, row, :, :, first : first + KW] = shapes[:, power][:, None, :]
    return table.reshape(POWERS, tile_rows, len(SIGMAS) * POWERS * height)


def gather_kernel(
    nexp,
    nccd,
    cap,
    shift_ref,
    science_hbm,
    variance_hbm,
    template_hbm,
    owner_hbm,
    slot_hbm,
    top_hbm,
    left_hbm,
    coeff_hbm,
    cols_hbm,
    rows_hbm,
    tiles_ref,
    codes_ref,
    tally_ref,
    science_ref,
    variance_ref,
    coeff_ref,
    cols_ref,
    rows_ref,
    stripe,
    metas,
    weights,
    load_sems,
    halo_send,
    halo_recv,
    far_sems,
    near_sems,
    sems,
):
    e = lax.axis_index("exp")
    c = lax.axis_index("ccd")
    count = nexp * nccd
    lanes = nccd // 2
    half = nexp * lanes
    parity = lax.rem(c, 2)
    mine = e * lanes + c // 2
    me = e * nccd + c
    rows = science_ref.shape[0]
    height = rows + 2 * HALO

    fields = (owner_hbm, slot_hbm, top_hbm, left_hbm)
    rows_of = owner_hbm.shape[0]
    pairs = [(template_hbm, stripe.at[0, pl.ds(HALO, rows)])]
    for index, field in enumerate(fields):
        pairs.append((field, metas.at[parity, mine, pl.ds(index * rows_of, rows_of)]))
    pairs += [
        (coeff_hbm, coeff_ref),
        (rows_hbm, rows_ref),
        (cols_hbm, cols_ref),
        (science_hbm, science_ref),
        (variance_hbm, variance_ref),
    ]
    loads = [
        pltpu.make_async_copy(source, target, load_sems.at[index])
        for index, (source, target) in enumerate(pairs)
    ]
    for load in loads:
        load.start()

    barrier = pltpu.get_barrier_semaphore()

    def greet(k, carry):
        other = lax.rem(me + k, count)
        pl.semaphore_signal(
            barrier, inc=1, device_id=(other // nccd, lax.rem(other, nccd)), device_id_type=MESH
        )
        return carry

    lax.fori_loop(1, count, greet, 0)

    @pl.when(c == 0)
    def _():
        stripe[:, pl.ds(0, HALO), :] = jnp.zeros((2, HALO, stripe.shape[2]), jnp.bfloat16)

    @pl.when(c == nccd - 1)
    def _():
        stripe[:, pl.ds(rows + HALO, HALO), :] = jnp.zeros(
            (2, HALO, stripe.shape[2]), jnp.bfloat16
        )

    for load in loads[:5]:
        load.wait()
    pl.semaphore_wait(barrier, count - 1)

    before = lax.rem(e + nexp - 1, nexp)

    def halo(index, src_row, size, side, dst_row, device):
        return pltpu.make_async_remote_copy(
            src_ref=stripe.at[0, pl.ds(HALO + src_row, size)],
            dst_ref=stripe.at[side, pl.ds(dst_row, size)],
            send_sem=halo_send.at[index],
            recv_sem=halo_recv.at[index],
            device_id=device,
            device_id_type=MESH,
        )

    full = halo(0, 0, rows, 1, HALO, (before, c))
    down = [
        halo(1, rows - HALO, HALO, 0, 0, (e, c + 1)),
        halo(2, rows - HALO, HALO, 1, 0, (before, c + 1)),
    ]
    up = [
        halo(3, 0, HALO, 0, rows + HALO, (e, c - 1)),
        halo(4, 0, HALO, 1, rows + HALO, (before, c - 1)),
    ]
    full.start()

    @pl.when(c < nccd - 1)
    def _():
        for copy in down:
            copy.start()

    @pl.when(c > 0)
    def _():
        for copy in up:
            copy.start()

    def spread(ref, send, recv):
        def body(k, carry):
            other = lax.rem(mine + k, half)
            pltpu.make_async_remote_copy(
                src_ref=ref.at[parity, mine],
                dst_ref=ref.at[parity, mine],
                send_sem=sems.at[send],
                recv_sem=sems.at[recv],
                device_id=(other // lanes, lax.rem(other, lanes) * 2 + parity),
                device_id_type=MESH,
            ).start()
            return carry

        lax.fori_loop(1, half, body, 0)

    def wait_spread(ref, sem):
        part = ref.at[0, pl.ds(0, half - 1)]
        pltpu.make_async_copy(part, part, sems.at[sem]).wait()

    def share(ref, send, recv):
        return pltpu.make_async_remote_copy(
            src_ref=ref.at[parity],
            dst_ref=ref.at[parity],
            send_sem=sems.at[send],
            recv_sem=sems.at[recv],
            device_id=(e, c + 1 - 2 * parity),
            device_id_type=MESH,
        )

    spread(metas, 0, 1)

    span = science_ref.shape[1]
    offset = shift_ref[0, 0] - MARGIN
    source = lax.broadcasted_iota(jnp.int32, (2 * span, 2 * span), 0)
    target = lax.broadcasted_iota(jnp.int32, (2 * span, 2 * span), 1)
    pick = (source == target + offset).astype(jnp.float32).astype(jnp.bfloat16)

    for load in loads[5:7]:
        load.wait()
    wide = rows_ref.shape[2]
    bases = coeff_ref.shape[1]
    basis = lax.broadcasted_iota(jnp.int32, (8, bases), 1)
    which = lax.broadcasted_iota(jnp.int32, (8, bases), 0)
    split = jnp.where((basis // POWERS) % POWERS == which, coeff_ref[...], 0.0)
    basis = lax.broadcasted_iota(jnp.int32, (bases, wide), 0)
    kind = lax.broadcasted_iota(jnp.int32, (bases, wide), 1) // height
    owns = (basis // (POWERS * POWERS)) * POWERS + basis % POWERS == kind
    spread_coeff = jnp.dot(
        split,
        owns.astype(jnp.float32),
        precision=lax.Precision.HIGHEST,
        preferred_element_type=jnp.float32,
    )
    total = jnp.zeros(rows_ref.shape[1:], jnp.float32)
    for power in range(POWERS):
        total = total + (rows_ref[power] * spread_coeff[power : power + 1]).astype(
            jnp.bfloat16
        ).astype(jnp.float32)
    high = total.astype(jnp.bfloat16)
    weights[pl.ds(0, rows), :] = high
    weights[pl.ds(rows, rows), :] = (total - high.astype(jnp.float32)).astype(jnp.bfloat16)

    for load in loads[7:]:
        load.wait()

    full.wait_recv()

    @pl.when(c > 0)
    def _():
        for copy in down:
            copy.wait_recv()

    @pl.when(c < nccd - 1)
    def _():
        for copy in up:
            copy.wait_recv()

    joined = jnp.concatenate([stripe[0], stripe[1]], axis=1)
    window = jnp.dot(joined, pick, preferred_element_type=jnp.float32).astype(jnp.bfloat16)
    smeared = jnp.dot(window, cols_ref[...], preferred_element_type=jnp.float32).astype(
        jnp.bfloat16
    )
    kinds = len(SIGMAS) * POWERS
    stacked = jnp.concatenate(
        [smeared[:, kind * span : (kind + 1) * span] for kind in range(kinds)], axis=0
    )
    both = jnp.dot(weights[...], stacked, preferred_element_type=jnp.float32)
    model = both[:rows] + both[rows:]
    snr = (science_ref[...] - model) / jnp.sqrt(variance_ref[...])
    tiles_ref[parity, mine] = snr.astype(jnp.bfloat16)

    plane = 2 * lanes
    groups = half // plane
    group = mine // plane
    place_in = lax.rem(mine, plane)

    def pass_on(slot, other, send, recv):
        return pltpu.make_async_remote_copy(
            src_ref=tiles_ref.at[parity, slot],
            dst_ref=tiles_ref.at[parity, slot],
            send_sem=send,
            recv_sem=recv,
            device_id=(other // lanes, lax.rem(other, lanes) * 2 + parity),
            device_id_type=MESH,
        )

    def to_plane(slot, number):
        for k in range(1, plane):
            other = group * plane + lax.rem(place_in + k, plane)
            pass_on(slot, other, sems.at[2], near_sems.at[number]).start()

    def start_far(k, carry):
        other = lax.rem(mine + k * plane, half)
        pass_on(mine, other, sems.at[3], far_sems.at[group]).start()
        return carry

    def wait_tiles(number, sem):
        part = tiles_ref.at[0, pl.ds(0, number)]
        pltpu.make_async_copy(part, part, sem).wait()

    def share_group(number):
        part = tiles_ref.at[parity, pl.ds(number * plane, plane)]
        return pltpu.make_async_remote_copy(
            src_ref=part,
            dst_ref=part,
            send_sem=sems.at[6],
            recv_sem=sems.at[7],
            device_id=(e, c + 1 - 2 * parity),
            device_id_type=MESH,
        )

    lax.fori_loop(1, groups, start_far, 0)
    to_plane(mine, group)

    def go_on(k, carry):
        number = lax.rem(group + k, groups)
        wait_tiles(1, far_sems.at[number])
        to_plane(number * plane + place_in, number)
        return carry

    lax.fori_loop(1, groups, go_on, 0)

    wait_spread(metas, 1)
    meta_share = share(metas, 4, 5)
    meta_share.start()
    meta_share.wait_recv()

    shape = (count, span)
    lower = lax.broadcasted_iota(jnp.int32, (span, span), 0)
    upper = lax.broadcasted_iota(jnp.int32, (span, span), 1)
    earlier = (lower < upper).astype(jnp.float32).astype(jnp.bfloat16)
    table = metas[...].reshape(count, metas.shape[2], span)
    seen = jnp.zeros((count, 1), jnp.float32)
    parts = []
    for part in range(rows_of):
        match = table[:, part, :] == me
        flags = match.astype(jnp.float32)
        place = seen + jnp.dot(
            flags.astype(jnp.bfloat16), earlier, preferred_element_type=jnp.float32
        )
        seen = seen + jnp.sum(flags, axis=1, keepdims=True)
        code = (
            (table[:, rows_of + part, :] + 1) * 8192
            + table[:, 2 * rows_of + part, :] * 128
            + table[:, 3 * rows_of + part, :]
        ).astype(jnp.float32)
        parts.append((jnp.where(match, place, -1.0), code))
    length = codes_ref.shape[1]
    tri = lax.broadcasted_iota(jnp.int32, (count, count), 1) < lax.broadcasted_iota(
        jnp.int32, (count, count), 0
    )
    starts = jnp.dot(
        tri.astype(jnp.float32).astype(jnp.bfloat16),
        jnp.broadcast_to(seen, shape).astype(jnp.bfloat16),
        preferred_element_type=jnp.float32,
    )[:, :1].astype(jnp.int32)
    ends = starts + seen.astype(jnp.int32)
    tile_row = lax.broadcasted_iota(jnp.int32, (count, 1), 0) * rows
    ahead = lax.broadcasted_iota(jnp.int32, (count, length), 1)
    ahead = jnp.where(ahead < ends, ahead - starts, -1)
    listing = jnp.zeros((count, length), jnp.int32)
    for entry in range(cap):
        found = sum(jnp.where(place == entry, code, 0.0) for place, code in parts)
        code = jnp.sum(found, axis=1, keepdims=True).astype(jnp.int32)
        code = (code >> 13) * 4194304 + (((code >> 7) & 63) + tile_row) * 128 + (code & 127)
        listing = jnp.where(ahead == entry, code, listing)
    listing = jnp.sum(listing, axis=0, keepdims=True)
    slots = lax.broadcasted_iota(jnp.int32, (OBJ_DEV, length), 0) + 1
    tally = jnp.sum((slots == (listing >> 22)).astype(jnp.float32), axis=1, keepdims=True)
    tally_ref[...] = jnp.broadcast_to(jnp.maximum(tally, 1.0), tally_ref.shape)
    codes_ref[...] = jnp.concatenate(
        [
            listing,
            jnp.broadcast_to(jnp.sum(seen.astype(jnp.int32), axis=0, keepdims=True), (1, length)),
        ],
        axis=0,
    )

    def hand_over(k, carry):
        number = lax.rem(group + k, groups)
        wait_tiles(plane - 1, near_sems.at[number])
        share_group(number).start()
        return carry

    lax.fori_loop(0, groups, hand_over, 0)
    wait_tiles(half, sems.at[7])

    full.wait_send()

    @pl.when(c < nccd - 1)
    def _():
        for copy in down:
            copy.wait_send()

    @pl.when(c > 0)
    def _():
        for copy in up:
            copy.wait_send()

    wait_spread(metas, 0)
    meta_share.wait_send()
    wait_tiles(groups - 1, sems.at[3])
    wait_tiles((plane - 1) * groups, sems.at[2])
    wait_tiles(half, sems.at[6])


GROUP = 16
PARTS = 4
PACK = 8


def stamp_kernel(codes_ref, tiles_ref, tally_ref, out_ref, wide, *sums):
    count, rows, span = tiles_ref.shape
    fold = span // CUT
    chunk_tiles = 4

    def widen(step, carry):
        for k in range(chunk_tiles):
            t = step * chunk_tiles + k
            wide[pl.ds(pl.multiple_of(t * rows, rows), rows), :] = tiles_ref[t].astype(
                jnp.float32
            )
        return carry

    lax.fori_loop(0, count // chunk_tiles, widen, 0)
    for part in sums:
        part[...] = jnp.zeros(part.shape, jnp.float32)
    lane = lax.broadcasted_iota(jnp.int32, (PACK, span), 1)

    def some(g, carry):
        cuts = []
        for k in range(GROUP):
            code = codes_ref[0, g * GROUP + k]
            top = (code >> 7) & 32767
            packed = None
            for q in range(fold):
                value = pltpu.roll(
                    wide[pl.ds(top + q * PACK, PACK), :],
                    (span + q * CUT - (code & 127)) & (span - 1),
                    1,
                )
                packed = value if q == 0 else jnp.where(lane >= q * CUT, value, packed)
            cuts.append((code >> 22, packed))
        for k, (slot, value) in enumerate(cuts):
            at = pl.ds(pl.multiple_of(slot * PACK, PACK), PACK)
            sums[k % PARTS][at, :] = sums[k % PARTS][at, :] + value
        return carry

    lax.fori_loop(0, (codes_ref[1, 0] + GROUP - 1) // GROUP, some, 0)
    sums[0][...] = (sums[0][...] + sums[1][...]) + (sums[2][...] + sums[3][...])

    def finish(block, carry):
        first = (block * 8 + 1) * PACK
        slots = pl.ds(pl.multiple_of(block * 8, 8), 8)
        tally = tally_ref[slots, :]
        lines = [sums[0][pl.ds(first + r, 8, stride=PACK), :] for r in range(PACK)]
        for q in range(fold):
            for h in range(PACK // fold):
                merged = None
                for k in range(fold):
                    line = lines[h * fold + k]
                    turn = ((k - q) * CUT) % span
                    line = pltpu.roll(line, turn, 1) if turn else line
                    merged = line if k == 0 else jnp.where(lane >= k * CUT, line, merged)
                chunk = q * (PACK // fold) + h
                out_ref[slots, pl.ds(chunk * span, span)] = merged / tally
        return carry

    lax.fori_loop(0, OBJ_DEV // 8, finish, 0)


def shards(
    nexp,
    nccd,
    science,
    variance,
    template,
    kernel_coeff,
    template_shift,
    corner_rows,
    corner_cols,
    owner_device,
    object_slot,
):
    rows, span = science.shape[1:]
    sources = object_slot.shape[-1]
    count = nexp * nccd
    half = count // 2
    cap = max(2, (2 * sources + count - 1) // count)
    fields = [
        part.reshape(sources // span, span)
        for part in (owner_device, object_slot, corner_rows, corner_cols)
    ]
    meta_shape = (4 * (sources // span), span)
    length = count * cap
    height = rows + 2 * HALO
    kinds = len(SIGMAS) * POWERS
    cols = jnp.asarray(column_table(span)).astype(jnp.bfloat16)
    downs = jnp.asarray(row_table(rows))
    vmem = pl.BlockSpec(memory_space=pltpu.VMEM)
    smem = pl.BlockSpec(memory_space=pltpu.SMEM)
    tiles, codes, tally = pl.pallas_call(
        functools.partial(gather_kernel, nexp, nccd, cap),
        out_shape=(
            jax.ShapeDtypeStruct((2, half, rows, span), jnp.bfloat16),
            jax.ShapeDtypeStruct((2, length), jnp.int32),
            jax.ShapeDtypeStruct((OBJ_DEV, span), jnp.float32),
        ),
        in_specs=[smem] + [pl.BlockSpec(memory_space=pl.ANY)] * 10,
        out_specs=(vmem, vmem, vmem),
        scratch_shapes=[
            pltpu.VMEM((rows, span), jnp.float32),
            pltpu.VMEM((rows, span), jnp.float32),
            pltpu.VMEM(kernel_coeff.shape[1:], jnp.float32),
            pltpu.VMEM(cols.shape, jnp.bfloat16),
            pltpu.VMEM(downs.shape, jnp.float32),
            pltpu.VMEM((2, height, span), jnp.bfloat16),
            pltpu.VMEM((2, half) + meta_shape, jnp.int32),
            pltpu.VMEM((2 * rows, kinds * height), jnp.bfloat16),
            pltpu.SemaphoreType.DMA((10,)),
            pltpu.SemaphoreType.DMA((5,)),
            pltpu.SemaphoreType.DMA((5,)),
            pltpu.SemaphoreType.DMA((nexp // 2,)),
            pltpu.SemaphoreType.DMA((nexp // 2,)),
            pltpu.SemaphoreType.DMA((8,)),
        ],
        compiler_params=pltpu.CompilerParams(
            collective_id=0, has_side_effects=True, vmem_limit_bytes=LIMIT
        ),
        name="snr_gather",
    )(
        template_shift,
        science[0],
        variance[0],
        template[0],
        *fields,
        kernel_coeff[0],
        cols,
        downs,
    )
    return pl.pallas_call(
        stamp_kernel,
        out_shape=jax.ShapeDtypeStruct((OBJ_DEV, CUT * CUT), jnp.float32),
        in_specs=[smem, vmem, vmem],
        out_specs=vmem,
        scratch_shapes=[
            pltpu.VMEM((count * rows, span), jnp.float32),
        ]
        + [pltpu.VMEM(((OBJ_DEV + 1) * PACK, span), jnp.float32)] * PARTS,
        compiler_params=pltpu.CompilerParams(vmem_limit_bytes=LIMIT),
        name="stamp_sums",
    )(codes, tiles.reshape(count, rows, span), tally)


def solution(mesh):
    placed = (
        P("exp", "ccd", None),
        P("exp", "ccd", None),
        P("exp", "ccd", None),
        P("exp", "ccd", None),
        P("exp", "ccd"),
        P("exp", "ccd", None),
        P("exp", "ccd", None),
        P("exp", "ccd", None, None),
        P("exp", "ccd", None),
    )
    return jax.shard_map(
        functools.partial(shards, mesh.shape["exp"], mesh.shape["ccd"]),
        mesh=mesh,
        in_specs=placed,
        out_specs=P(("exp", "ccd"), None),
        check_vma=False,
    )
```

```python
import functools

import jax
import jax.numpy as jnp
import numpy as np
from jax import lax
from jax.experimental import pallas as pl
from jax.experimental.pallas import tpu as pltpu
from jax.sharding import PartitionSpec as P

KW = 21
CUT = 32
OBJ_DEV = 128
HALO = 16
MARGIN = KW // 2
SIGMAS = (1.0, 2.0, 3.5)
POWERS = 4
MESH = pl.DeviceIdType.MESH
LIMIT = 60 * 1024 * 1024


def profiles():
    offsets = np.arange(KW) - MARGIN
    out = np.zeros((len(SIGMAS), POWERS, KW))
    for group, sigma in enumerate(SIGMAS):
        scaled = offsets / sigma
        for power in range(POWERS):
            value = scaled**power * np.exp(-0.5 * scaled * scaled)
            out[group, power] = value / np.sqrt(np.sum(value * value))
    return out


def column_table(span):
    table = np.zeros((2 * span, len(SIGMAS) * POWERS * span), np.float32)
    shapes = profiles().reshape(-1, KW)
    for index, shape in enumerate(shapes):
        for column in range(span):
            table[column : column + KW, index * span + column] = shape
    return table


def row_table(tile_rows):
    height = tile_rows + 2 * HALO
    table = np.zeros((POWERS, tile_rows, len(SIGMAS), POWERS, height), np.float32)
    shapes = profiles().astype(np.float32)
    for power in range(POWERS):
        for row in range(tile_rows):
            first = row + HALO - MARGIN
            table[power, row, :, :, first : first + KW] = shapes[:, power][:, None, :]
    return table.reshape(POWERS, tile_rows, len(SIGMAS) * POWERS * height)


def gather_kernel(
    nexp,
    nccd,
    cap,
    shift_ref,
    science_hbm,
    variance_hbm,
    template_hbm,
    owner_hbm,
    slot_hbm,
    top_hbm,
    left_hbm,
    coeff_hbm,
    cols_hbm,
    rows_hbm,
    tiles_ref,
    codes_ref,
    tally_ref,
    science_ref,
    variance_ref,
    coeff_ref,
    cols_ref,
    rows_ref,
    stripe,
    metas,
    weights,
    load_sems,
    halo_send,
    halo_recv,
    near_sems,
    sems,
):
    e = lax.axis_index("exp")
    c = lax.axis_index("ccd")
    count = nexp * nccd
    lanes = nccd // 2
    half = nexp * lanes
    parity = lax.rem(c, 2)
    mine = e * lanes + c // 2
    me = e * nccd + c
    rows = science_ref.shape[0]
    height = rows + 2 * HALO

    fields = (owner_hbm, slot_hbm, top_hbm, left_hbm)
    rows_of = owner_hbm.shape[0]
    pairs = [(template_hbm, stripe.at[0, pl.ds(HALO, rows)])]
    for index, field in enumerate(fields):
        pairs.append((field, metas.at[parity, mine, pl.ds(index * rows_of, rows_of)]))
    pairs += [
        (coeff_hbm, coeff_ref),
        (rows_hbm, rows_ref),
        (cols_hbm, cols_ref),
        (science_hbm, science_ref),
        (variance_hbm, variance_ref),
    ]
    loads = [
        pltpu.make_async_copy(source, target, load_sems.at[index])
        for index, (source, target) in enumerate(pairs)
    ]
    for load in loads:
        load.start()

    barrier = pltpu.get_barrier_semaphore()

    def greet(k, carry):
        other = lax.rem(me + k, count)
        pl.semaphore_signal(
            barrier, inc=1, device_id=(other // nccd, lax.rem(other, nccd)), device_id_type=MESH
        )
        return carry

    lax.fori_loop(1, count, greet, 0)

    @pl.when(c == 0)
    def _():
        stripe[:, pl.ds(0, HALO), :] = jnp.zeros((2, HALO, stripe.shape[2]), jnp.bfloat16)

    @pl.when(c == nccd - 1)
    def _():
        stripe[:, pl.ds(rows + HALO, HALO), :] = jnp.zeros(
            (2, HALO, stripe.shape[2]), jnp.bfloat16
        )

    for load in loads[:5]:
        load.wait()
    pl.semaphore_wait(barrier, count - 1)

    before = lax.rem(e + nexp - 1, nexp)

    def halo(index, src_row, size, side, dst_row, device):
        return pltpu.make_async_remote_copy(
            src_ref=stripe.at[0, pl.ds(HALO + src_row, size)],
            dst_ref=stripe.at[side, pl.ds(dst_row, size)],
            send_sem=halo_send.at[index],
            recv_sem=halo_recv.at[index],
            device_id=device,
            device_id_type=MESH,
        )

    full = halo(0, 0, rows, 1, HALO, (before, c))
    down = [
        halo(1, rows - HALO, HALO, 0, 0, (e, c + 1)),
        halo(2, rows - HALO, HALO, 1, 0, (before, c + 1)),
    ]
    up = [
        halo(3, 0, HALO, 0, rows + HALO, (e, c - 1)),
        halo(4, 0, HALO, 1, rows + HALO, (before, c - 1)),
    ]
    full.start()

    @pl.when(c < nccd - 1)
    def _():
        for copy in down:
            copy.start()

    @pl.when(c > 0)
    def _():
        for copy in up:
            copy.start()

    def spread(ref, send, recv):
        def body(k, carry):
            other = lax.rem(mine + k, half)
            pltpu.make_async_remote_copy(
                src_ref=ref.at[parity, mine],
                dst_ref=ref.at[parity, mine],
                send_sem=sems.at[send],
                recv_sem=sems.at[recv],
                device_id=(other // lanes, lax.rem(other, lanes) * 2 + parity),
                device_id_type=MESH,
            ).start()
            return carry

        lax.fori_loop(1, half, body, 0)

    def wait_spread(ref, sem):
        part = ref.at[0, pl.ds(0, half - 1)]
        pltpu.make_async_copy(part, part, sems.at[sem]).wait()

    def share(ref, send, recv):
        return pltpu.make_async_remote_copy(
            src_ref=ref.at[parity],
            dst_ref=ref.at[parity],
            send_sem=sems.at[send],
            recv_sem=sems.at[recv],
            device_id=(e, c + 1 - 2 * parity),
            device_id_type=MESH,
        )

    spread(metas, 0, 1)

    span = science_ref.shape[1]
    offset = shift_ref[0, 0] - MARGIN
    source = lax.broadcasted_iota(jnp.int32, (2 * span, 2 * span), 0)
    target = lax.broadcasted_iota(jnp.int32, (2 * span, 2 * span), 1)
    pick = (source == target + offset).astype(jnp.float32).astype(jnp.bfloat16)

    for load in loads[5:7]:
        load.wait()
    wide = rows_ref.shape[2]
    bases = coeff_ref.shape[1]
    basis = lax.broadcasted_iota(jnp.int32, (8, bases), 1)
    which = lax.broadcasted_iota(jnp.int32, (8, bases), 0)
    split = jnp.where((basis // POWERS) % POWERS == which, coeff_ref[...], 0.0)
    basis = lax.broadcasted_iota(jnp.int32, (bases, wide), 0)
    kind = lax.broadcasted_iota(jnp.int32, (bases, wide), 1) // height
    owns = (basis // (POWERS * POWERS)) * POWERS + basis % POWERS == kind
    spread_coeff = jnp.dot(
        split,
        owns.astype(jnp.float32),
        precision=lax.Precision.HIGHEST,
        preferred_element_type=jnp.float32,
    )
    total = jnp.zeros(rows_ref.shape[1:], jnp.float32)
    for power in range(POWERS):
        total = total + (rows_ref[power] * spread_coeff[power : power + 1]).astype(
            jnp.bfloat16
        ).astype(jnp.float32)
    high = total.astype(jnp.bfloat16)
    weights[pl.ds(0, rows), :] = high
    weights[pl.ds(rows, rows), :] = (total - high.astype(jnp.float32)).astype(jnp.bfloat16)

    for load in loads[7:]:
        load.wait()

    full.wait_recv()

    @pl.when(c > 0)
    def _():
        for copy in down:
            copy.wait_recv()

    @pl.when(c < nccd - 1)
    def _():
        for copy in up:
            copy.wait_recv()

    joined = jnp.concatenate([stripe[0], stripe[1]], axis=1)
    window = jnp.dot(joined, pick, preferred_element_type=jnp.float32).astype(jnp.bfloat16)
    smeared = jnp.dot(window, cols_ref[...], preferred_element_type=jnp.float32).astype(
        jnp.bfloat16
    )
    kinds = len(SIGMAS) * POWERS
    stacked = jnp.concatenate(
        [smeared[:, kind * span : (kind + 1) * span] for kind in range(kinds)], axis=0
    )
    both = jnp.dot(weights[...], stacked, preferred_element_type=jnp.float32)
    model = both[:rows] + both[rows:]
    snr = (science_ref[...] - model) / jnp.sqrt(variance_ref[...])
    tiles_ref[parity, mine] = snr.astype(jnp.bfloat16)

    plane = 2 * lanes
    groups = half // plane
    group = mine // plane

    def send_tile(k, carry):
        other = lax.rem(mine + k, half)
        pltpu.make_async_remote_copy(
            src_ref=tiles_ref.at[parity, mine],
            dst_ref=tiles_ref.at[parity, mine],
            send_sem=sems.at[2],
            recv_sem=near_sems.at[group],
            device_id=(other // lanes, lax.rem(other, lanes) * 2 + parity),
            device_id_type=MESH,
        ).start()
        return carry

    def wait_tiles(number, sem):
        part = tiles_ref.at[0, pl.ds(0, number)]
        pltpu.make_async_copy(part, part, sem).wait()

    def share_group(number):
        part = tiles_ref.at[parity, pl.ds(number * plane, plane)]
        return pltpu.make_async_remote_copy(
            src_ref=part,
            dst_ref=part,
            send_sem=sems.at[6],
            recv_sem=sems.at[7],
            device_id=(e, c + 1 - 2 * parity),
            device_id_type=MESH,
        )

    lax.fori_loop(1, half, send_tile, 0)

    wait_spread(metas, 1)
    meta_share = share(metas, 4, 5)
    meta_share.start()
    meta_share.wait_recv()

    shape = (count, span)
    lower = lax.broadcasted_iota(jnp.int32, (span, span), 0)
    upper = lax.broadcasted_iota(jnp.int32, (span, span), 1)
    earlier = (lower < upper).astype(jnp.float32).astype(jnp.bfloat16)
    table = metas[...].reshape(count, metas.shape[2], span)
    seen = jnp.zeros((count, 1), jnp.float32)
    parts = []
    for part in range(rows_of):
        match = table[:, part, :] == me
        flags = match.astype(jnp.float32)
        place = seen + jnp.dot(
            flags.astype(jnp.bfloat16), earlier, preferred_element_type=jnp.float32
        )
        seen = seen + jnp.sum(flags, axis=1, keepdims=True)
        code = (
            (table[:, rows_of + part, :] + 1) * 8192
            + table[:, 2 * rows_of + part, :] * 128
            + table[:, 3 * rows_of + part, :]
        ).astype(jnp.float32)
        parts.append((jnp.where(match, place, -1.0), code))
    length = codes_ref.shape[1]
    tri = lax.broadcasted_iota(jnp.int32, (count, count), 1) < lax.broadcasted_iota(
        jnp.int32, (count, count), 0
    )
    starts = jnp.dot(
        tri.astype(jnp.float32).astype(jnp.bfloat16),
        jnp.broadcast_to(seen, shape).astype(jnp.bfloat16),
        preferred_element_type=jnp.float32,
    )[:, :1].astype(jnp.int32)
    ends = starts + seen.astype(jnp.int32)
    tile_row = lax.broadcasted_iota(jnp.int32, (count, 1), 0) * rows
    ahead = lax.broadcasted_iota(jnp.int32, (count, length), 1)
    ahead = jnp.where(ahead < ends, ahead - starts, -1)
    listing = jnp.zeros((count, length), jnp.int32)
    for entry in range(cap):
        found = sum(jnp.where(place == entry, code, 0.0) for place, code in parts)
        code = jnp.sum(found, axis=1, keepdims=True).astype(jnp.int32)
        code = (code >> 13) * 4194304 + (((code >> 7) & 63) + tile_row) * 128 + (code & 127)
        listing = jnp.where(ahead == entry, code, listing)
    listing = jnp.sum(listing, axis=0, keepdims=True)
    slots = lax.broadcasted_iota(jnp.int32, (OBJ_DEV, length), 0) + 1
    tally = jnp.sum((slots == (listing >> 22)).astype(jnp.float32), axis=1, keepdims=True)
    tally_ref[...] = jnp.broadcast_to(jnp.maximum(tally, 1.0), tally_ref.shape)
    codes_ref[...] = jnp.concatenate(
        [
            listing,
            jnp.broadcast_to(jnp.sum(seen.astype(jnp.int32), axis=0, keepdims=True), (1, length)),
        ],
        axis=0,
    )

    wait_tiles(plane - 1, near_sems.at[group])
    share_group(group).start()

    def hand_over(k, carry):
        number = lax.rem(group + groups - k, groups)
        wait_tiles(plane, near_sems.at[number])
        share_group(number).start()
        return carry

    lax.fori_loop(1, groups, hand_over, 0)
    wait_tiles(half, sems.at[7])

    full.wait_send()

    @pl.when(c < nccd - 1)
    def _():
        for copy in down:
            copy.wait_send()

    @pl.when(c > 0)
    def _():
        for copy in up:
            copy.wait_send()

    wait_spread(metas, 0)
    meta_share.wait_send()
    wait_tiles(half - 1, sems.at[2])
    wait_tiles(half, sems.at[6])


GROUP = 16
PARTS = 4
PACK = 8


def stamp_kernel(codes_ref, tiles_ref, tally_ref, out_ref, wide, *sums):
    count, rows, span = tiles_ref.shape
    fold = span // CUT
    chunk_tiles = 4

    def widen(step, carry):
        for k in range(chunk_tiles):
            t = step * chunk_tiles + k
            wide[pl.ds(pl.multiple_of(t * rows, rows), rows), :] = tiles_ref[t].astype(
                jnp.float32
            )
        return carry

    lax.fori_loop(0, count // chunk_tiles, widen, 0)
    for part in sums:
        part[...] = jnp.zeros(part.shape, jnp.float32)
    lane = lax.broadcasted_iota(jnp.int32, (PACK, span), 1)

    def some(g, carry):
        cuts = []
        for k in range(GROUP):
            code = codes_ref[0, g * GROUP + k]
            top = (code >> 7) & 32767
            packed = None
            for q in range(fold):
                value = pltpu.roll(
                    wide[pl.ds(top + q * PACK, PACK), :],
                    (span + q * CUT - (code & 127)) & (span - 1),
                    1,
                )
                packed = value if q == 0 else jnp.where(lane >= q * CUT, value, packed)
            cuts.append((code >> 22, packed))
        for k, (slot, value) in enumerate(cuts):
            at = pl.ds(pl.multiple_of(slot * PACK, PACK), PACK)
            sums[k % PARTS][at, :] = sums[k % PARTS][at, :] + value
        return carry

    lax.fori_loop(0, (codes_ref[1, 0] + GROUP - 1) // GROUP, some, 0)
    sums[0][...] = (sums[0][...] + sums[1][...]) + (sums[2][...] + sums[3][...])

    def finish(block, carry):
        first = (block * 8 + 1) * PACK
        slots = pl.ds(pl.multiple_of(block * 8, 8), 8)
        tally = tally_ref[slots, :]
        lines = [sums[0][pl.ds(first + r, 8, stride=PACK), :] for r in range(PACK)]
        for q in range(fold):
            for h in range(PACK // fold):
                merged = None
                for k in range(fold):
                    line = lines[h * fold + k]
                    turn = ((k - q) * CUT) % span
                    line = pltpu.roll(line, turn, 1) if turn else line
                    merged = line if k == 0 else jnp.where(lane >= k * CUT, line, merged)
                chunk = q * (PACK // fold) + h
                out_ref[slots, pl.ds(chunk * span, span)] = merged / tally
        return carry

    lax.fori_loop(0, OBJ_DEV // 8, finish, 0)


def shards(
    nexp,
    nccd,
    science,
    variance,
    template,
    kernel_coeff,
    template_shift,
    corner_rows,
    corner_cols,
    owner_device,
    object_slot,
):
    rows, span = science.shape[1:]
    sources = object_slot.shape[-1]
    count = nexp * nccd
    half = count // 2
    cap = max(2, (2 * sources + count - 1) // count)
    fields = [
        part.reshape(sources // span, span)
        for part in (owner_device, object_slot, corner_rows, corner_cols)
    ]
    meta_shape = (4 * (sources // span), span)
    length = count * cap
    height = rows + 2 * HALO
    kinds = len(SIGMAS) * POWERS
    cols = jnp.asarray(column_table(span)).astype(jnp.bfloat16)
    downs = jnp.asarray(row_table(rows))
    vmem = pl.BlockSpec(memory_space=pltpu.VMEM)
    smem = pl.BlockSpec(memory_space=pltpu.SMEM)
    tiles, codes, tally = pl.pallas_call(
        functools.partial(gather_kernel, nexp, nccd, cap),
        out_shape=(
            jax.ShapeDtypeStruct((2, half, rows, span), jnp.bfloat16),
            jax.ShapeDtypeStruct((2, length), jnp.int32),
            jax.ShapeDtypeStruct((OBJ_DEV, span), jnp.float32),
        ),
        in_specs=[smem] + [pl.BlockSpec(memory_space=pl.ANY)] * 10,
        out_specs=(vmem, vmem, vmem),
        scratch_shapes=[
            pltpu.VMEM((rows, span), jnp.float32),
            pltpu.VMEM((rows, span), jnp.float32),
            pltpu.VMEM(kernel_coeff.shape[1:], jnp.float32),
            pltpu.VMEM(cols.shape, jnp.bfloat16),
            pltpu.VMEM(downs.shape, jnp.float32),
            pltpu.VMEM((2, height, span), jnp.bfloat16),
            pltpu.VMEM((2, half) + meta_shape, jnp.int32),
            pltpu.VMEM((2 * rows, kinds * height), jnp.bfloat16),
            pltpu.SemaphoreType.DMA((10,)),
            pltpu.SemaphoreType.DMA((5,)),
            pltpu.SemaphoreType.DMA((5,)),
            pltpu.SemaphoreType.DMA((nexp // 2,)),
            pltpu.SemaphoreType.DMA((8,)),
        ],
        compiler_params=pltpu.CompilerParams(
            collective_id=0, has_side_effects=True, vmem_limit_bytes=LIMIT
        ),
        name="snr_gather",
    )(
        template_shift,
        science[0],
        variance[0],
        template[0],
        *fields,
        kernel_coeff[0],
        cols,
        downs,
    )
    return pl.pallas_call(
        stamp_kernel,
        out_shape=jax.ShapeDtypeStruct((OBJ_DEV, CUT * CUT), jnp.float32),
        in_specs=[smem, vmem, vmem],
        out_specs=vmem,
        scratch_shapes=[
            pltpu.VMEM((count * rows, span), jnp.float32),
        ]
        + [pltpu.VMEM(((OBJ_DEV + 1) * PACK, span), jnp.float32)] * PARTS,
        compiler_params=pltpu.CompilerParams(vmem_limit_bytes=LIMIT),
        name="stamp_sums",
    )(codes, tiles.reshape(count, rows, span), tally)


def solution(mesh):
    placed = (
        P("exp", "ccd", None),
        P("exp", "ccd", None),
        P("exp", "ccd", None),
        P("exp", "ccd", None),
        P("exp", "ccd"),
        P("exp", "ccd", None),
        P("exp", "ccd", None),
        P("exp", "ccd", None, None),
        P("exp", "ccd", None),
    )
    return jax.shard_map(
        functools.partial(shards, mesh.shape["exp"], mesh.shape["ccd"]),
        mesh=mesh,
        in_specs=placed,
        out_specs=P(("exp", "ccd"), None),
        check_vma=False,
    )
```

```python
import functools

import jax
import jax.numpy as jnp
import numpy as np
from jax import lax
from jax.experimental import pallas as pl
from jax.experimental.pallas import tpu as pltpu
from jax.sharding import PartitionSpec as P

KW = 21
CUT = 32
OBJ_DEV = 128
HALO = 16
MARGIN = KW // 2
SIGMAS = (1.0, 2.0, 3.5)
POWERS = 4
MESH = pl.DeviceIdType.MESH
LIMIT = 60 * 1024 * 1024


def profiles():
    offsets = np.arange(KW) - MARGIN
    out = np.zeros((len(SIGMAS), POWERS, KW))
    for group, sigma in enumerate(SIGMAS):
        scaled = offsets / sigma
        for power in range(POWERS):
            value = scaled**power * np.exp(-0.5 * scaled * scaled)
            out[group, power] = value / np.sqrt(np.sum(value * value))
    return out


def column_table(span):
    table = np.zeros((2 * span, len(SIGMAS) * POWERS * span), np.float32)
    shapes = profiles().reshape(-1, KW)
    for index, shape in enumerate(shapes):
        for column in range(span):
            table[column : column + KW, index * span + column] = shape
    return table


def row_table(tile_rows):
    height = tile_rows + 2 * HALO
    table = np.zeros((POWERS, tile_rows, len(SIGMAS), POWERS, height), np.float32)
    shapes = profiles().astype(np.float32)
    for power in range(POWERS):
        for row in range(tile_rows):
            first = row + HALO - MARGIN
            table[power, row, :, :, first : first + KW] = shapes[:, power][:, None, :]
    return table.reshape(POWERS, tile_rows, len(SIGMAS) * POWERS * height)


def gather_kernel(
    nexp,
    nccd,
    cap,
    shift_ref,
    science_hbm,
    variance_hbm,
    template_hbm,
    owner_hbm,
    slot_hbm,
    top_hbm,
    left_hbm,
    coeff_hbm,
    cols_hbm,
    rows_hbm,
    tiles_ref,
    codes_ref,
    tally_ref,
    science_ref,
    variance_ref,
    coeff_ref,
    cols_ref,
    rows_ref,
    stripe,
    metas,
    weights,
    load_sems,
    halo_send,
    halo_recv,
    near_sems,
    sems,
):
    e = lax.axis_index("exp")
    c = lax.axis_index("ccd")
    count = nexp * nccd
    lanes = nccd // 2
    half = nexp * lanes
    parity = lax.rem(c, 2)
    mine = e * lanes + c // 2
    me = e * nccd + c
    rows = science_ref.shape[0]
    height = rows + 2 * HALO

    fields = (owner_hbm, slot_hbm, top_hbm, left_hbm)
    rows_of = owner_hbm.shape[0]
    pairs = [(template_hbm, stripe.at[0, pl.ds(HALO, rows)])]
    for index, field in enumerate(fields):
        pairs.append((field, metas.at[parity, mine, pl.ds(index * rows_of, rows_of)]))
    pairs += [
        (coeff_hbm, coeff_ref),
        (rows_hbm, rows_ref),
        (cols_hbm, cols_ref),
        (science_hbm, science_ref),
        (variance_hbm, variance_ref),
    ]
    loads = [
        pltpu.make_async_copy(source, target, load_sems.at[index])
        for index, (source, target) in enumerate(pairs)
    ]
    for load in loads:
        load.start()

    barrier = pltpu.get_barrier_semaphore()

    def greet(k, carry):
        other = lax.rem(me + k, count)
        pl.semaphore_signal(
            barrier, inc=1, device_id=(other // nccd, lax.rem(other, nccd)), device_id_type=MESH
        )
        return carry

    lax.fori_loop(1, count, greet, 0)

    @pl.when(c == 0)
    def _():
        stripe[:, pl.ds(0, HALO), :] = jnp.zeros((2, HALO, stripe.shape[2]), jnp.bfloat16)

    @pl.when(c == nccd - 1)
    def _():
        stripe[:, pl.ds(rows + HALO, HALO), :] = jnp.zeros(
            (2, HALO, stripe.shape[2]), jnp.bfloat16
        )

    for load in loads[:5]:
        load.wait()
    pl.semaphore_wait(barrier, count - 1)

    before = lax.rem(e + nexp - 1, nexp)

    def halo(index, src_row, size, side, dst_row, device):
        return pltpu.make_async_remote_copy(
            src_ref=stripe.at[0, pl.ds(HALO + src_row, size)],
            dst_ref=stripe.at[side, pl.ds(dst_row, size)],
            send_sem=halo_send.at[index],
            recv_sem=halo_recv.at[index],
            device_id=device,
            device_id_type=MESH,
        )

    full = halo(0, 0, rows, 1, HALO, (before, c))
    down = [
        halo(1, rows - HALO, HALO, 0, 0, (e, c + 1)),
        halo(2, rows - HALO, HALO, 1, 0, (before, c + 1)),
    ]
    up = [
        halo(3, 0, HALO, 0, rows + HALO, (e, c - 1)),
        halo(4, 0, HALO, 1, rows + HALO, (before, c - 1)),
    ]
    full.start()

    @pl.when(c < nccd - 1)
    def _():
        for copy in down:
            copy.start()

    @pl.when(c > 0)
    def _():
        for copy in up:
            copy.start()

    def spread(ref, send, recv):
        def body(k, carry):
            other = lax.rem(mine + k, half)
            pltpu.make_async_remote_copy(
                src_ref=ref.at[parity, mine],
                dst_ref=ref.at[parity, mine],
                send_sem=sems.at[send],
                recv_sem=sems.at[recv],
                device_id=(other // lanes, lax.rem(other, lanes) * 2 + parity),
                device_id_type=MESH,
            ).start()
            return carry

        lax.fori_loop(1, half, body, 0)

    def wait_spread(ref, sem):
        part = ref.at[0, pl.ds(0, half - 1)]
        pltpu.make_async_copy(part, part, sems.at[sem]).wait()

    def share(ref, send, recv):
        return pltpu.make_async_remote_copy(
            src_ref=ref.at[parity],
            dst_ref=ref.at[parity],
            send_sem=sems.at[send],
            recv_sem=sems.at[recv],
            device_id=(e, c + 1 - 2 * parity),
            device_id_type=MESH,
        )

    spread(metas, 0, 1)

    span = science_ref.shape[1]
    offset = shift_ref[0, 0] - MARGIN
    source = lax.broadcasted_iota(jnp.int32, (2 * span, 2 * span), 0)
    target = lax.broadcasted_iota(jnp.int32, (2 * span, 2 * span), 1)
    pick = (source == target + offset).astype(jnp.float32).astype(jnp.bfloat16)

    for load in loads[5:7]:
        load.wait()
    wide = rows_ref.shape[2]
    bases = coeff_ref.shape[1]
    basis = lax.broadcasted_iota(jnp.int32, (8, bases), 1)
    which = lax.broadcasted_iota(jnp.int32, (8, bases), 0)
    split = jnp.where((basis // POWERS) % POWERS == which, coeff_ref[...], 0.0)
    basis = lax.broadcasted_iota(jnp.int32, (bases, wide), 0)
    kind = lax.broadcasted_iota(jnp.int32, (bases, wide), 1) // height
    owns = (basis // (POWERS * POWERS)) * POWERS + basis % POWERS == kind
    spread_coeff = jnp.dot(
        split,
        owns.astype(jnp.float32),
        precision=lax.Precision.HIGHEST,
        preferred_element_type=jnp.float32,
    )
    total = jnp.zeros(rows_ref.shape[1:], jnp.float32)
    for power in range(POWERS):
        total = total + (rows_ref[power] * spread_coeff[power : power + 1]).astype(
            jnp.bfloat16
        ).astype(jnp.float32)
    high = total.astype(jnp.bfloat16)
    weights[pl.ds(0, rows), :] = high
    weights[pl.ds(rows, rows), :] = (total - high.astype(jnp.float32)).astype(jnp.bfloat16)

    for load in loads[7:]:
        load.wait()

    full.wait_recv()

    @pl.when(c > 0)
    def _():
        for copy in down:
            copy.wait_recv()

    @pl.when(c < nccd - 1)
    def _():
        for copy in up:
            copy.wait_recv()

    joined = jnp.concatenate([stripe[0], stripe[1]], axis=1)
    window = jnp.dot(joined, pick, preferred_element_type=jnp.float32).astype(jnp.bfloat16)
    smeared = jnp.dot(window, cols_ref[...], preferred_element_type=jnp.float32).astype(
        jnp.bfloat16
    )
    kinds = len(SIGMAS) * POWERS
    stacked = jnp.concatenate(
        [smeared[:, kind * span : (kind + 1) * span] for kind in range(kinds)], axis=0
    )
    both = jnp.dot(weights[...], stacked, preferred_element_type=jnp.float32)
    model = both[:rows] + both[rows:]
    snr = (science_ref[...] - model) / jnp.sqrt(variance_ref[...])
    tiles_ref[parity, mine] = snr.astype(jnp.bfloat16)

    plane = 2 * lanes
    groups = half // plane
    group = mine // plane

    def send_tile(k, carry):
        other = lax.rem(mine + k, half)
        pltpu.make_async_remote_copy(
            src_ref=tiles_ref.at[parity, mine],
            dst_ref=tiles_ref.at[parity, mine],
            send_sem=sems.at[2],
            recv_sem=near_sems.at[group],
            device_id=(other // lanes, lax.rem(other, lanes) * 2 + parity),
            device_id_type=MESH,
        ).start()
        return carry

    def wait_tiles(number, sem):
        part = tiles_ref.at[0, pl.ds(0, number)]
        pltpu.make_async_copy(part, part, sem).wait()

    def share_group(number):
        part = tiles_ref.at[parity, pl.ds(number * plane, plane)]
        return pltpu.make_async_remote_copy(
            src_ref=part,
            dst_ref=part,
            send_sem=sems.at[6],
            recv_sem=sems.at[7],
            device_id=(e, c + 1 - 2 * parity),
            device_id_type=MESH,
        )

    lax.fori_loop(1, half, send_tile, 0)

    wait_spread(metas, 1)
    meta_share = share(metas, 4, 5)
    meta_share.start()
    meta_share.wait_recv()

    shape = (count, span)
    lower = lax.broadcasted_iota(jnp.int32, (span, span), 0)
    upper = lax.broadcasted_iota(jnp.int32, (span, span), 1)
    earlier = (lower < upper).astype(jnp.float32).astype(jnp.bfloat16)
    table = metas[...].reshape(count, metas.shape[2], span)
    seen = jnp.zeros((count, 1), jnp.float32)
    parts = []
    for part in range(rows_of):
        match = table[:, part, :] == me
        flags = match.astype(jnp.float32)
        place = seen + jnp.dot(
            flags.astype(jnp.bfloat16), earlier, preferred_element_type=jnp.float32
        )
        seen = seen + jnp.sum(flags, axis=1, keepdims=True)
        code = (
            (table[:, rows_of + part, :] + 1) * 8192
            + table[:, 2 * rows_of + part, :] * 128
            + table[:, 3 * rows_of + part, :]
        ).astype(jnp.float32)
        parts.append((jnp.where(match, place, -1.0), code))
    length = codes_ref.shape[1]
    tri = lax.broadcasted_iota(jnp.int32, (count, count), 1) < lax.broadcasted_iota(
        jnp.int32, (count, count), 0
    )
    starts = jnp.dot(
        tri.astype(jnp.float32).astype(jnp.bfloat16),
        jnp.broadcast_to(seen, shape).astype(jnp.bfloat16),
        preferred_element_type=jnp.float32,
    )[:, :1].astype(jnp.int32)
    ends = starts + seen.astype(jnp.int32)
    tile_row = lax.broadcasted_iota(jnp.int32, (count, 1), 0) * rows
    ahead = lax.broadcasted_iota(jnp.int32, (count, length), 1)
    ahead = jnp.where(ahead < ends, ahead - starts, -1)
    listing = jnp.zeros((count, length), jnp.int32)
    for entry in range(cap):
        found = sum(jnp.where(place == entry, code, 0.0) for place, code in parts)
        code = jnp.sum(found, axis=1, keepdims=True).astype(jnp.int32)
        code = (code >> 13) * 4194304 + (((code >> 7) & 63) + tile_row) * 128 + (code & 127)
        listing = jnp.where(ahead == entry, code, listing)
    listing = jnp.sum(listing, axis=0, keepdims=True)
    slots = lax.broadcasted_iota(jnp.int32, (OBJ_DEV, length), 0) + 1
    tally = jnp.sum((slots == (listing >> 22)).astype(jnp.float32), axis=1, keepdims=True)
    tally_ref[...] = jnp.broadcast_to(jnp.maximum(tally, 1.0), tally_ref.shape)
    codes_ref[...] = jnp.concatenate(
        [
            listing,
            jnp.broadcast_to(jnp.sum(seen.astype(jnp.int32), axis=0, keepdims=True), (1, length)),
        ],
        axis=0,
    )

    wait_tiles(plane - 1, near_sems.at[group])
    share_group(group).start()

    def hand_over(k, carry):
        number = lax.rem(group + groups - k, groups)
        wait_tiles(plane, near_sems.at[number])
        share_group(number).start()
        return carry

    lax.fori_loop(1, groups, hand_over, 0)
    wait_tiles(half, sems.at[7])

    full.wait_send()

    @pl.when(c < nccd - 1)
    def _():
        for copy in down:
            copy.wait_send()

    @pl.when(c > 0)
    def _():
        for copy in up:
            copy.wait_send()

    wait_spread(metas, 0)
    meta_share.wait_send()
    wait_tiles(half - 1, sems.at[2])
    wait_tiles(half, sems.at[6])


GROUP = 32
PARTS = 4
PACK = 8


def stamp_kernel(codes_ref, tiles_ref, tally_ref, out_ref, wide, *sums):
    count, rows, span = tiles_ref.shape
    fold = span // CUT
    chunk_tiles = 4

    def widen(step, carry):
        for k in range(chunk_tiles):
            t = step * chunk_tiles + k
            wide[pl.ds(pl.multiple_of(t * rows, rows), rows), :] = tiles_ref[t].astype(
                jnp.float32
            )
        return carry

    lax.fori_loop(0, count // chunk_tiles, widen, 0)
    for part in sums:
        part[...] = jnp.zeros(part.shape, jnp.float32)
    lane = lax.broadcasted_iota(jnp.int32, (PACK, span), 1)

    def some(g, carry):
        cuts = []
        for k in range(GROUP):
            code = codes_ref[0, g * GROUP + k]
            top = (code >> 7) & 32767
            packed = None
            for q in range(fold):
                value = pltpu.roll(
                    wide[pl.ds(top + q * PACK, PACK), :],
                    (span + q * CUT - (code & 127)) & (span - 1),
                    1,
                )
                packed = value if q == 0 else jnp.where(lane >= q * CUT, value, packed)
            cuts.append((code >> 22, packed))
        for k, (slot, value) in enumerate(cuts):
            at = pl.ds(pl.multiple_of(slot * PACK, PACK), PACK)
            sums[k % PARTS][at, :] = sums[k % PARTS][at, :] + value
        return carry

    lax.fori_loop(0, (codes_ref[1, 0] + GROUP - 1) // GROUP, some, 0)
    sums[0][...] = (sums[0][...] + sums[1][...]) + (sums[2][...] + sums[3][...])

    def finish(block, carry):
        first = (block * 8 + 1) * PACK
        slots = pl.ds(pl.multiple_of(block * 8, 8), 8)
        tally = tally_ref[slots, :]
        lines = [sums[0][pl.ds(first + r, 8, stride=PACK), :] for r in range(PACK)]
        for q in range(fold):
            for h in range(PACK // fold):
                merged = None
                for k in range(fold):
                    line = lines[h * fold + k]
                    turn = ((k - q) * CUT) % span
                    line = pltpu.roll(line, turn, 1) if turn else line
                    merged = line if k == 0 else jnp.where(lane >= k * CUT, line, merged)
                chunk = q * (PACK // fold) + h
                out_ref[slots, pl.ds(chunk * span, span)] = merged / tally
        return carry

    lax.fori_loop(0, OBJ_DEV // 8, finish, 0)


def shards(
    nexp,
    nccd,
    science,
    variance,
    template,
    kernel_coeff,
    template_shift,
    corner_rows,
    corner_cols,
    owner_device,
    object_slot,
):
    rows, span = science.shape[1:]
    sources = object_slot.shape[-1]
    count = nexp * nccd
    half = count // 2
    cap = max(2, (2 * sources + count - 1) // count)
    fields = [
        part.reshape(sources // span, span)
        for part in (owner_device, object_slot, corner_rows, corner_cols)
    ]
    meta_shape = (4 * (sources // span), span)
    length = count * cap
    height = rows + 2 * HALO
    kinds = len(SIGMAS) * POWERS
    cols = jnp.asarray(column_table(span)).astype(jnp.bfloat16)
    downs = jnp.asarray(row_table(rows))
    vmem = pl.BlockSpec(memory_space=pltpu.VMEM)
    smem = pl.BlockSpec(memory_space=pltpu.SMEM)
    tiles, codes, tally = pl.pallas_call(
        functools.partial(gather_kernel, nexp, nccd, cap),
        out_shape=(
            jax.ShapeDtypeStruct((2, half, rows, span), jnp.bfloat16),
            jax.ShapeDtypeStruct((2, length), jnp.int32),
            jax.ShapeDtypeStruct((OBJ_DEV, span), jnp.float32),
        ),
        in_specs=[smem] + [pl.BlockSpec(memory_space=pl.ANY)] * 10,
        out_specs=(vmem, vmem, vmem),
        scratch_shapes=[
            pltpu.VMEM((rows, span), jnp.float32),
            pltpu.VMEM((rows, span), jnp.float32),
            pltpu.VMEM(kernel_coeff.shape[1:], jnp.float32),
            pltpu.VMEM(cols.shape, jnp.bfloat16),
            pltpu.VMEM(downs.shape, jnp.float32),
            pltpu.VMEM((2, height, span), jnp.bfloat16),
            pltpu.VMEM((2, half) + meta_shape, jnp.int32),
            pltpu.VMEM((2 * rows, kinds * height), jnp.bfloat16),
            pltpu.SemaphoreType.DMA((10,)),
            pltpu.SemaphoreType.DMA((5,)),
            pltpu.SemaphoreType.DMA((5,)),
            pltpu.SemaphoreType.DMA((nexp // 2,)),
            pltpu.SemaphoreType.DMA((8,)),
        ],
        compiler_params=pltpu.CompilerParams(
            collective_id=0, has_side_effects=True, vmem_limit_bytes=LIMIT
        ),
        name="snr_gather",
    )(
        template_shift,
        science[0],
        variance[0],
        template[0],
        *fields,
        kernel_coeff[0],
        cols,
        downs,
    )
    return pl.pallas_call(
        stamp_kernel,
        out_shape=jax.ShapeDtypeStruct((OBJ_DEV, CUT * CUT), jnp.float32),
        in_specs=[smem, vmem, vmem],
        out_specs=vmem,
        scratch_shapes=[
            pltpu.VMEM((count * rows, span), jnp.float32),
        ]
        + [pltpu.VMEM(((OBJ_DEV + 1) * PACK, span), jnp.float32)] * PARTS,
        compiler_params=pltpu.CompilerParams(vmem_limit_bytes=LIMIT),
        name="stamp_sums",
    )(codes, tiles.reshape(count, rows, span), tally)


def solution(mesh):
    placed = (
        P("exp", "ccd", None),
        P("exp", "ccd", None),
        P("exp", "ccd", None),
        P("exp", "ccd", None),
        P("exp", "ccd"),
        P("exp", "ccd", None),
        P("exp", "ccd", None),
        P("exp", "ccd", None, None),
        P("exp", "ccd", None),
    )
    return jax.shard_map(
        functools.partial(shards, mesh.shape["exp"], mesh.shape["ccd"]),
        mesh=mesh,
        in_specs=placed,
        out_specs=P(("exp", "ccd"), None),
        check_vma=False,
    )
```

```python
import functools

import jax
import jax.numpy as jnp
import numpy as np
from jax import lax
from jax.experimental import pallas as pl
from jax.experimental.pallas import tpu as pltpu
from jax.sharding import PartitionSpec as P

KW = 21
CUT = 32
OBJ_DEV = 128
HALO = 16
MARGIN = KW // 2
SIGMAS = (1.0, 2.0, 3.5)
POWERS = 4
MESH = pl.DeviceIdType.MESH
LIMIT = 60 * 1024 * 1024


def profiles():
    offsets = np.arange(KW) - MARGIN
    out = np.zeros((len(SIGMAS), POWERS, KW))
    for group, sigma in enumerate(SIGMAS):
        scaled = offsets / sigma
        for power in range(POWERS):
            value = scaled**power * np.exp(-0.5 * scaled * scaled)
            out[group, power] = value / np.sqrt(np.sum(value * value))
    return out


def column_table(span):
    table = np.zeros((2 * span, len(SIGMAS) * POWERS * span), np.float32)
    shapes = profiles().reshape(-1, KW)
    for index, shape in enumerate(shapes):
        for column in range(span):
            table[column : column + KW, index * span + column] = shape
    return table


def row_table(tile_rows):
    height = tile_rows + 2 * HALO
    table = np.zeros((POWERS, tile_rows, len(SIGMAS), POWERS, height), np.float32)
    shapes = profiles().astype(np.float32)
    for power in range(POWERS):
        for row in range(tile_rows):
            first = row + HALO - MARGIN
            table[power, row, :, :, first : first + KW] = shapes[:, power][:, None, :]
    return table.reshape(POWERS, tile_rows, len(SIGMAS) * POWERS * height)


def gather_kernel(
    nexp,
    nccd,
    cap,
    shift_ref,
    science_hbm,
    variance_hbm,
    template_hbm,
    owner_hbm,
    slot_hbm,
    top_hbm,
    left_hbm,
    coeff_hbm,
    cols_hbm,
    rows_hbm,
    tiles_ref,
    codes_ref,
    tally_ref,
    science_ref,
    variance_ref,
    coeff_ref,
    cols_ref,
    rows_ref,
    stripe,
    metas,
    weights,
    load_sems,
    halo_send,
    halo_recv,
    near_sems,
    sems,
):
    e = lax.axis_index("exp")
    c = lax.axis_index("ccd")
    count = nexp * nccd
    lanes = nccd // 2
    half = nexp * lanes
    parity = lax.rem(c, 2)
    mine = e * lanes + c // 2
    me = e * nccd + c
    rows = science_ref.shape[0]
    height = rows + 2 * HALO

    fields = (owner_hbm, slot_hbm, top_hbm, left_hbm)
    rows_of = owner_hbm.shape[0]
    pairs = [(template_hbm, stripe.at[0, pl.ds(HALO, rows)])]
    for index, field in enumerate(fields):
        pairs.append((field, metas.at[parity, mine, pl.ds(index * rows_of, rows_of)]))
    pairs += [
        (coeff_hbm, coeff_ref),
        (rows_hbm, rows_ref),
        (cols_hbm, cols_ref),
        (science_hbm, science_ref),
        (variance_hbm, variance_ref),
    ]
    loads = [
        pltpu.make_async_copy(source, target, load_sems.at[index])
        for index, (source, target) in enumerate(pairs)
    ]
    for load in loads:
        load.start()

    barrier = pltpu.get_barrier_semaphore()

    def greet(k, carry):
        other = lax.rem(me + k, count)
        pl.semaphore_signal(
            barrier, inc=1, device_id=(other // nccd, lax.rem(other, nccd)), device_id_type=MESH
        )
        return carry

    lax.fori_loop(1, count, greet, 0)

    @pl.when(c == 0)
    def _():
        stripe[:, pl.ds(0, HALO), :] = jnp.zeros((2, HALO, stripe.shape[2]), jnp.bfloat16)

    @pl.when(c == nccd - 1)
    def _():
        stripe[:, pl.ds(rows + HALO, HALO), :] = jnp.zeros(
            (2, HALO, stripe.shape[2]), jnp.bfloat16
        )

    for load in loads[:5]:
        load.wait()
    pl.semaphore_wait(barrier, count - 1)

    before = lax.rem(e + nexp - 1, nexp)

    def halo(index, src_row, size, side, dst_row, device):
        return pltpu.make_async_remote_copy(
            src_ref=stripe.at[0, pl.ds(HALO + src_row, size)],
            dst_ref=stripe.at[side, pl.ds(dst_row, size)],
            send_sem=halo_send.at[index],
            recv_sem=halo_recv.at[index],
            device_id=device,
            device_id_type=MESH,
        )

    full = halo(0, 0, rows, 1, HALO, (before, c))
    down = [
        halo(1, rows - HALO, HALO, 0, 0, (e, c + 1)),
        halo(2, rows - HALO, HALO, 1, 0, (before, c + 1)),
    ]
    up = [
        halo(3, 0, HALO, 0, rows + HALO, (e, c - 1)),
        halo(4, 0, HALO, 1, rows + HALO, (before, c - 1)),
    ]
    full.start()

    @pl.when(c < nccd - 1)
    def _():
        for copy in down:
            copy.start()

    @pl.when(c > 0)
    def _():
        for copy in up:
            copy.start()

    def spread(ref, send, recv):
        def body(k, carry):
            other = lax.rem(mine + k, half)
            pltpu.make_async_remote_copy(
                src_ref=ref.at[parity, mine],
                dst_ref=ref.at[parity, mine],
                send_sem=sems.at[send],
                recv_sem=sems.at[recv],
                device_id=(other // lanes, lax.rem(other, lanes) * 2 + parity),
                device_id_type=MESH,
            ).start()
            return carry

        lax.fori_loop(1, half, body, 0)

    def wait_spread(ref, sem):
        part = ref.at[0, pl.ds(0, half - 1)]
        pltpu.make_async_copy(part, part, sems.at[sem]).wait()

    def share(ref, send, recv):
        return pltpu.make_async_remote_copy(
            src_ref=ref.at[parity],
            dst_ref=ref.at[parity],
            send_sem=sems.at[send],
            recv_sem=sems.at[recv],
            device_id=(e, c + 1 - 2 * parity),
            device_id_type=MESH,
        )

    spread(metas, 0, 1)

    span = science_ref.shape[1]
    offset = shift_ref[0, 0] - MARGIN
    source = lax.broadcasted_iota(jnp.int32, (2 * span, 2 * span), 0)
    target = lax.broadcasted_iota(jnp.int32, (2 * span, 2 * span), 1)
    pick = (source == target + offset).astype(jnp.float32).astype(jnp.bfloat16)

    for load in loads[5:7]:
        load.wait()
    wide = rows_ref.shape[2]
    bases = coeff_ref.shape[1]
    basis = lax.broadcasted_iota(jnp.int32, (8, bases), 1)
    which = lax.broadcasted_iota(jnp.int32, (8, bases), 0)
    split = jnp.where((basis // POWERS) % POWERS == which, coeff_ref[...], 0.0)
    basis = lax.broadcasted_iota(jnp.int32, (bases, wide), 0)
    kind = lax.broadcasted_iota(jnp.int32, (bases, wide), 1) // height
    owns = (basis // (POWERS * POWERS)) * POWERS + basis % POWERS == kind
    spread_coeff = jnp.dot(
        split,
        owns.astype(jnp.float32),
        precision=lax.Precision.HIGHEST,
        preferred_element_type=jnp.float32,
    )
    total = jnp.zeros(rows_ref.shape[1:], jnp.float32)
    for power in range(POWERS):
        total = total + (rows_ref[power] * spread_coeff[power : power + 1]).astype(
            jnp.bfloat16
        ).astype(jnp.float32)
    high = total.astype(jnp.bfloat16)
    weights[pl.ds(0, rows), :] = high
    weights[pl.ds(rows, rows), :] = (total - high.astype(jnp.float32)).astype(jnp.bfloat16)

    for load in loads[7:]:
        load.wait()

    full.wait_recv()

    @pl.when(c > 0)
    def _():
        for copy in down:
            copy.wait_recv()

    @pl.when(c < nccd - 1)
    def _():
        for copy in up:
            copy.wait_recv()

    joined = jnp.concatenate([stripe[0], stripe[1]], axis=1)
    window = jnp.dot(joined, pick, preferred_element_type=jnp.float32).astype(jnp.bfloat16)
    smeared = jnp.dot(window, cols_ref[...], preferred_element_type=jnp.float32).astype(
        jnp.bfloat16
    )
    kinds = len(SIGMAS) * POWERS
    stacked = jnp.concatenate(
        [smeared[:, kind * span : (kind + 1) * span] for kind in range(kinds)], axis=0
    )
    both = jnp.dot(weights[...], stacked, preferred_element_type=jnp.float32)
    model = both[:rows] + both[rows:]
    snr = (science_ref[...] - model) / jnp.sqrt(variance_ref[...])
    tiles_ref[parity, mine] = snr.astype(jnp.bfloat16)

    plane = 2 * lanes
    groups = half // plane
    group = mine // plane

    def send_tile(k, carry):
        step = lax.rem(k - 1 + half // 2 - 1, half - 1) + 1
        other = lax.rem(mine + step, half)
        pltpu.make_async_remote_copy(
            src_ref=tiles_ref.at[parity, mine],
            dst_ref=tiles_ref.at[parity, mine],
            send_sem=sems.at[2],
            recv_sem=near_sems.at[group],
            device_id=(other // lanes, lax.rem(other, lanes) * 2 + parity),
            device_id_type=MESH,
        ).start()
        return carry

    def wait_tiles(number, sem):
        part = tiles_ref.at[0, pl.ds(0, number)]
        pltpu.make_async_copy(part, part, sem).wait()

    def share_group(number):
        part = tiles_ref.at[parity, pl.ds(number * plane, plane)]
        return pltpu.make_async_remote_copy(
            src_ref=part,
            dst_ref=part,
            send_sem=sems.at[6],
            recv_sem=sems.at[7],
            device_id=(e, c + 1 - 2 * parity),
            device_id_type=MESH,
        )

    lax.fori_loop(1, half, send_tile, 0)

    wait_spread(metas, 1)
    meta_share = share(metas, 4, 5)
    meta_share.start()
    meta_share.wait_recv()

    shape = (count, span)
    lower = lax.broadcasted_iota(jnp.int32, (span, span), 0)
    upper = lax.broadcasted_iota(jnp.int32, (span, span), 1)
    earlier = (lower < upper).astype(jnp.float32).astype(jnp.bfloat16)
    table = metas[...].reshape(count, metas.shape[2], span)
    seen = jnp.zeros((count, 1), jnp.float32)
    parts = []
    for part in range(rows_of):
        match = table[:, part, :] == me
        flags = match.astype(jnp.float32)
        place = seen + jnp.dot(
            flags.astype(jnp.bfloat16), earlier, preferred_element_type=jnp.float32
        )
        seen = seen + jnp.sum(flags, axis=1, keepdims=True)
        code = (
            (table[:, rows_of + part, :] + 1) * 8192
            + table[:, 2 * rows_of + part, :] * 128
            + table[:, 3 * rows_of + part, :]
        ).astype(jnp.float32)
        parts.append((jnp.where(match, place, -1.0), code))
    length = codes_ref.shape[1]
    tri = lax.broadcasted_iota(jnp.int32, (count, count), 1) < lax.broadcasted_iota(
        jnp.int32, (count, count), 0
    )
    starts = jnp.dot(
        tri.astype(jnp.float32).astype(jnp.bfloat16),
        jnp.broadcast_to(seen, shape).astype(jnp.bfloat16),
        preferred_element_type=jnp.float32,
    )[:, :1].astype(jnp.int32)
    ends = starts + seen.astype(jnp.int32)
    tile_row = lax.broadcasted_iota(jnp.int32, (count, 1), 0) * rows
    ahead = lax.broadcasted_iota(jnp.int32, (count, length), 1)
    ahead = jnp.where(ahead < ends, ahead - starts, -1)
    listing = jnp.zeros((count, length), jnp.int32)
    for entry in range(cap):
        found = sum(jnp.where(place == entry, code, 0.0) for place, code in parts)
        code = jnp.sum(found, axis=1, keepdims=True).astype(jnp.int32)
        code = (code >> 13) * 4194304 + (((code >> 7) & 63) + tile_row) * 128 + (code & 127)
        listing = jnp.where(ahead == entry, code, listing)
    listing = jnp.sum(listing, axis=0, keepdims=True)
    slots = lax.broadcasted_iota(jnp.int32, (OBJ_DEV, length), 0) + 1
    tally = jnp.sum((slots == (listing >> 22)).astype(jnp.float32), axis=1, keepdims=True)
    tally_ref[...] = jnp.broadcast_to(jnp.maximum(tally, 1.0), tally_ref.shape)
    codes_ref[...] = jnp.concatenate(
        [
            listing,
            jnp.broadcast_to(jnp.sum(seen.astype(jnp.int32), axis=0, keepdims=True), (1, length)),
        ],
        axis=0,
    )

    def hand_over(k, carry):
        step = lax.rem(k - 1 + groups // 2 - 1, groups - 1) + 1
        number = lax.rem(group + groups - step, groups)
        wait_tiles(plane, near_sems.at[number])
        share_group(number).start()
        return carry

    lax.fori_loop(1, groups, hand_over, 0)
    wait_tiles(plane - 1, near_sems.at[group])
    share_group(group).start()
    wait_tiles(half, sems.at[7])

    full.wait_send()

    @pl.when(c < nccd - 1)
    def _():
        for copy in down:
            copy.wait_send()

    @pl.when(c > 0)
    def _():
        for copy in up:
            copy.wait_send()

    wait_spread(metas, 0)
    meta_share.wait_send()
    wait_tiles(half - 1, sems.at[2])
    wait_tiles(half, sems.at[6])


GROUP = 32
PARTS = 4
PACK = 8


def stamp_kernel(codes_ref, tiles_ref, tally_ref, out_ref, wide, *sums):
    count, rows, span = tiles_ref.shape
    fold = span // CUT
    chunk_tiles = 4

    def widen(step, carry):
        for k in range(chunk_tiles):
            t = step * chunk_tiles + k
            wide[pl.ds(pl.multiple_of(t * rows, rows), rows), :] = tiles_ref[t].astype(
                jnp.float32
            )
        return carry

    lax.fori_loop(0, count // chunk_tiles, widen, 0)
    for part in sums:
        part[...] = jnp.zeros(part.shape, jnp.float32)
    lane = lax.broadcasted_iota(jnp.int32, (PACK, span), 1)

    def some(g, carry):
        cuts = []
        for k in range(GROUP):
            code = codes_ref[0, g * GROUP + k]
            top = (code >> 7) & 32767
            packed = None
            for q in range(fold):
                value = pltpu.roll(
                    wide[pl.ds(top + q * PACK, PACK), :],
                    (span + q * CUT - (code & 127)) & (span - 1),
                    1,
                )
                packed = value if q == 0 else jnp.where(lane >= q * CUT, value, packed)
            cuts.append((code >> 22, packed))
        for k, (slot, value) in enumerate(cuts):
            at = pl.ds(pl.multiple_of(slot * PACK, PACK), PACK)
            sums[k % PARTS][at, :] = sums[k % PARTS][at, :] + value
        return carry

    lax.fori_loop(0, (codes_ref[1, 0] + GROUP - 1) // GROUP, some, 0)
    sums[0][...] = (sums[0][...] + sums[1][...]) + (sums[2][...] + sums[3][...])

    def finish(block, carry):
        first = (block * 8 + 1) * PACK
        slots = pl.ds(pl.multiple_of(block * 8, 8), 8)
        tally = tally_ref[slots, :]
        lines = [sums[0][pl.ds(first + r, 8, stride=PACK), :] for r in range(PACK)]
        for q in range(fold):
            for h in range(PACK // fold):
                merged = None
                for k in range(fold):
                    line = lines[h * fold + k]
                    turn = ((k - q) * CUT) % span
                    line = pltpu.roll(line, turn, 1) if turn else line
                    merged = line if k == 0 else jnp.where(lane >= k * CUT, line, merged)
                chunk = q * (PACK // fold) + h
                out_ref[slots, pl.ds(chunk * span, span)] = merged / tally
        return carry

    lax.fori_loop(0, OBJ_DEV // 8, finish, 0)


def shards(
    nexp,
    nccd,
    science,
    variance,
    template,
    kernel_coeff,
    template_shift,
    corner_rows,
    corner_cols,
    owner_device,
    object_slot,
):
    rows, span = science.shape[1:]
    sources = object_slot.shape[-1]
    count = nexp * nccd
    half = count // 2
    cap = max(2, (2 * sources + count - 1) // count)
    fields = [
        part.reshape(sources // span, span)
        for part in (owner_device, object_slot, corner_rows, corner_cols)
    ]
    meta_shape = (4 * (sources // span), span)
    length = count * cap
    height = rows + 2 * HALO
    kinds = len(SIGMAS) * POWERS
    cols = jnp.asarray(column_table(span)).astype(jnp.bfloat16)
    downs = jnp.asarray(row_table(rows))
    vmem = pl.BlockSpec(memory_space=pltpu.VMEM)
    smem = pl.BlockSpec(memory_space=pltpu.SMEM)
    tiles, codes, tally = pl.pallas_call(
        functools.partial(gather_kernel, nexp, nccd, cap),
        out_shape=(
            jax.ShapeDtypeStruct((2, half, rows, span), jnp.bfloat16),
            jax.ShapeDtypeStruct((2, length), jnp.int32),
            jax.ShapeDtypeStruct((OBJ_DEV, span), jnp.float32),
        ),
        in_specs=[smem] + [pl.BlockSpec(memory_space=pl.ANY)] * 10,
        out_specs=(vmem, vmem, vmem),
        scratch_shapes=[
            pltpu.VMEM((rows, span), jnp.float32),
            pltpu.VMEM((rows, span), jnp.float32),
            pltpu.VMEM(kernel_coeff.shape[1:], jnp.float32),
            pltpu.VMEM(cols.shape, jnp.bfloat16),
            pltpu.VMEM(downs.shape, jnp.float32),
            pltpu.VMEM((2, height, span), jnp.bfloat16),
            pltpu.VMEM((2, half) + meta_shape, jnp.int32),
            pltpu.VMEM((2 * rows, kinds * height), jnp.bfloat16),
            pltpu.SemaphoreType.DMA((10,)),
            pltpu.SemaphoreType.DMA((5,)),
            pltpu.SemaphoreType.DMA((5,)),
            pltpu.SemaphoreType.DMA((nexp // 2,)),
            pltpu.SemaphoreType.DMA((8,)),
        ],
        compiler_params=pltpu.CompilerParams(
            collective_id=0, has_side_effects=True, vmem_limit_bytes=LIMIT
        ),
        name="snr_gather",
    )(
        template_shift,
        science[0],
        variance[0],
        template[0],
        *fields,
        kernel_coeff[0],
        cols,
        downs,
    )
    return pl.pallas_call(
        stamp_kernel,
        out_shape=jax.ShapeDtypeStruct((OBJ_DEV, CUT * CUT), jnp.float32),
        in_specs=[smem, vmem, vmem],
        out_specs=vmem,
        scratch_shapes=[
            pltpu.VMEM((count * rows, span), jnp.float32),
        ]
        + [pltpu.VMEM(((OBJ_DEV + 1) * PACK, span), jnp.float32)] * PARTS,
        compiler_params=pltpu.CompilerParams(vmem_limit_bytes=LIMIT),
        name="stamp_sums",
    )(codes, tiles.reshape(count, rows, span), tally)


def solution(mesh):
    placed = (
        P("exp", "ccd", None),
        P("exp", "ccd", None),
        P("exp", "ccd", None),
        P("exp", "ccd", None),
        P("exp", "ccd"),
        P("exp", "ccd", None),
        P("exp", "ccd", None),
        P("exp", "ccd", None, None),
        P("exp", "ccd", None),
    )
    return jax.shard_map(
        functools.partial(shards, mesh.shape["exp"], mesh.shape["ccd"]),
        mesh=mesh,
        in_specs=placed,
        out_specs=P(("exp", "ccd"), None),
        check_vma=False,
    )
```
